512 devices in a mesh: dp: 64 (over z, x), tensor: 8 (over y, core).
Axes of the slice: x: 4, y: 4, z: 16, core: 2. Of those that a mesh axis runs over, the one named last changes fastest.
Arguments:
- decode_input_rows: bfloat16 [8192, 12288], P('dp', 'tensor'), may hold values from -6 to 6
- decode_adapter_index: int32 [8192], P('dp'), may hold values from 0 to 127, as said below
- adapter_storage_index: int32 [128], replicated, may hold values from 0 to 127, as said below
- learner_input_rows: bfloat16 [8192, 12288], P('dp', 'tensor'), may hold values from -6 to 6
- learner_gradient: bfloat16 [8192, 28672], P('dp', 'tensor'), may hold values from -6 to 6
- block_adapter_index: int32 [64], P('dp'), may hold values from 0 to 127, as said below
- block_live_count: int32 [64], P('dp'), may hold values from 16 to 128, as said below
- adapter_down_weight: bfloat16 [128, 64, 12288], P('dp', None, 'tensor'), may hold values from -6 to 6
- adapter_up_weight: bfloat16 [128, 64, 28672], P('dp', None, 'tensor'), may hold values from -6 to 6
Outputs:
- dec_delta: bfloat16 [8192, 28672], P('dp', 'tensor')
- refreshed_down_weight: bfloat16 [128, 64, 12288], P('dp', None, 'tensor')
- refreshed_up_weight: bfloat16 [128, 64, 28672], P('dp', None, 'tensor')
The draws below stay inside these ranges and needn't reach their ends.
Inputs may be any that keep to these rules, and one draw needn't show every extreme that they name: A permutation. Adapter a is stored at index adapter_storage_index[a] of adapter_down_weight and adapter_up_weight, and the dp index adapter_storage_index[a] // 2 owns it. `decode_adapter_index`: among the rows of one dp index, at most 4 name adapters of one owner. In every draw one owner gets exactly 4 from every dp index. Each dp index also sends exactly 4 to a second owner, which may differ from index to index. `block_adapter_index`: each block names an adapter owned by the dp index that holds the block. The live rows of a block are its first block_live_count rows; the others are padding.
All inputs are finite; a program needn't handle non-finite values.
Results may differ from the reference program's by a relative error of at most 0.0049.
Values may be sent and summed in bfloat16 or wider, within the bound.
A program may use at most 64 MiB of HBM per device.

```python
import jax
import jax.numpy as jnp
from jax import lax

MODEL_WIDTH = 12288
HIDDEN_UNITS = 28672
ADAPTER_RANK = 64
ADAPTERS_PER_DP = 2
BLOCK = 128
ROLL_DEV = 128
LB_DEV = 1
ADAPTER_COUNT = 128
ROLL = 8192
LTOK = 8192
N_DP = 64


def shared_tables(key):
    slot_of = jax.random.permutation(jax.random.fold_in(key, 101), ADAPTER_COUNT).astype(jnp.int32)
    adapter_at = jnp.argsort(slot_of).astype(jnp.int32)
    busy = jax.random.permutation(jax.random.fold_in(key, 102), N_DP).astype(jnp.int32)
    return (slot_of, adapter_at, busy)


def draw_adapter_storage_index(key, part):
    return shared_tables(key)[0]


def draw_decode_adapter_index(key, part):
    slot_of, adapter_at, busy = shared_tables(key)
    key = jax.random.fold_in(key, 7)
    depth = 2 * ROLL_DEV // N_DP
    pool = jnp.arange(N_DP * depth, dtype=jnp.int32)

    def one_block(sub):
        first_key, order_key, shuffle_key, local_key = jax.random.split(sub, 4)
        heavy = busy[0]
        second = busy[1 + jax.random.randint(first_key, (), 0, min(3, N_DP - 1))]
        owner_of = pool // depth
        ranks = jax.random.permutation(order_key, N_DP * depth).astype(jnp.int32)
        score = jnp.where(owner_of == heavy, pool % depth - 2 * depth, jnp.where(owner_of == second, pool % depth - depth, ranks))
        taken = pool[jnp.argsort(score)][:ROLL_DEV]
        taken = jax.random.permutation(shuffle_key, taken)
        local_slot = jax.random.randint(local_key, (ROLL_DEV,), 0, ADAPTERS_PER_DP)
        return adapter_at[taken // depth * ADAPTERS_PER_DP + local_slot]
    picked = jax.vmap(one_block)(jax.random.split(key, N_DP))
    return picked.reshape(-1).astype(jnp.int32)


def draw_block_adapter_index(key, part):
    slot_of, adapter_at, busy = shared_tables(key)
    key = jax.random.fold_in(key, 8)
    owner_of = jnp.arange(N_DP * LB_DEV, dtype=jnp.int32) // LB_DEV
    local_slot = jax.random.randint(key, (N_DP * LB_DEV,), 0, ADAPTERS_PER_DP)
    return adapter_at[owner_of * ADAPTERS_PER_DP + local_slot].astype(jnp.int32)


def draw_block_live_count(key, part):
    key = jax.random.fold_in(key, 9)
    fills = jax.random.randint(key, (N_DP * LB_DEV,), BLOCK // 8, BLOCK + 1)
    fills = fills.at[0].set(BLOCK).at[1].set(BLOCK // 8)
    return fills.astype(jnp.int32)


def steps_of(stream_key, extent, cuts, smallest, largest):
    level, own = 1.0, jax.random.fold_in(stream_key, 6)
    for position, parts in cuts:
        draws = jnp.exp(jax.random.uniform(jax.random.fold_in(own, position), (parts,), jnp.float32, smallest / len(cuts), largest / len(cuts)))
        level = level * jnp.repeat(draws, extent[position] // parts).reshape([-1 if axis == position else 1 for axis in range(len(extent))])
    return level


def noise(rng, dims, spread, most, cuts=(), kind=jnp.bfloat16):
    drawn = spread * jax.random.normal(rng, dims, jnp.float32)
    if cuts:
        drawn = drawn * steps_of(rng, dims, cuts, -0.22, 0.18)
    return jnp.clip(drawn, -most, most).astype(kind)


def setup_inputs(seed: int = 0) -> dict:
    splits = jax.random.split(jax.random.key(seed), 10)
    return {
        "decode_input_rows": noise(splits[0], (ROLL, MODEL_WIDTH), 1.0, 6.0, ((0, 64), (1, 8))),
        "decode_adapter_index": draw_decode_adapter_index(jax.random.fold_in(splits[9], 71), 0),
        "adapter_storage_index": draw_adapter_storage_index(jax.random.fold_in(splits[9], 71), 0),
        "learner_input_rows": noise(splits[3], (LTOK, MODEL_WIDTH), 1.0, 6.0, ((0, 64), (1, 8))),
        "learner_gradient": noise(splits[4], (LTOK, HIDDEN_UNITS), 1.0, 6.0, ((0, 64), (1, 8))),
        "block_adapter_index": draw_block_adapter_index(jax.random.fold_in(splits[9], 71), 0),
        "block_live_count": draw_block_live_count(jax.random.fold_in(splits[9], 71), 0),
        "adapter_down_weight": noise(splits[7], (ADAPTER_COUNT, ADAPTER_RANK, MODEL_WIDTH), 1.0, 6.0, ((0, 64), (2, 8))),
        "adapter_up_weight": noise(splits[8], (ADAPTER_COUNT, ADAPTER_RANK, HIDDEN_UNITS), 1.0, 6.0, ((0, 64), (2, 8))),
    }


down_learning_rate = 4.0
up_learning_rate = 0.25


def reference(decode_input_rows, decode_adapter_index, adapter_storage_index, learner_input_rows, learner_gradient, block_adapter_index, block_live_count, adapter_down_weight, adapter_up_weight):
    shrink = MODEL_WIDTH ** -0.5
    expand = ADAPTER_RANK ** -0.5
    dec_slot = adapter_storage_index[decode_adapter_index].astype(jnp.int32)

    def decode_group(pieces):
        rows_in, incoming_storage_index = pieces
        gathered_down_weight = adapter_down_weight[incoming_storage_index].astype(jnp.float32)
        hidden = jnp.einsum("nd,nrd->nr", rows_in.astype(jnp.float32), gathered_down_weight) * shrink
        hidden = lax.optimization_barrier(hidden.astype(jnp.bfloat16)).astype(jnp.float32)
        gathered_up_weight = adapter_up_weight[incoming_storage_index].astype(jnp.float32)
        return (jnp.einsum("nr,nrf->nf", hidden, gathered_up_weight) * expand).astype(jnp.bfloat16)

    groups = ROLL // 32
    dec_delta = lax.map(decode_group, (decode_input_rows.reshape(groups, 32, MODEL_WIDTH), dec_slot.reshape(groups, 32)))
    dec_delta = dec_delta.reshape(ROLL, HIDDEN_UNITS)

    def owner_update(owner_index):
        first = owner_index * (LB_DEV * BLOCK)
        rows_b = lax.dynamic_slice_in_dim(learner_input_rows, first, LB_DEV * BLOCK, 0).reshape(LB_DEV, BLOCK, MODEL_WIDTH).astype(jnp.float32)
        grad_in = lax.dynamic_slice_in_dim(learner_gradient, first, LB_DEV * BLOCK, 0).reshape(LB_DEV, BLOCK, HIDDEN_UNITS).astype(jnp.float32)
        owner_ids = lax.dynamic_slice_in_dim(block_adapter_index, owner_index * LB_DEV, LB_DEV, 0)
        fills = lax.dynamic_slice_in_dim(block_live_count, owner_index * LB_DEV, LB_DEV, 0)
        owned_down_weight = lax.dynamic_slice_in_dim(adapter_down_weight, owner_index * ADAPTERS_PER_DP, ADAPTERS_PER_DP, 0)
        owned_up_weight = lax.dynamic_slice_in_dim(adapter_up_weight, owner_index * ADAPTERS_PER_DP, ADAPTERS_PER_DP, 0)
        local_slot = (adapter_storage_index[owner_ids] - owner_index * ADAPTERS_PER_DP).astype(jnp.int32)
        gather_down_weight = owned_down_weight[local_slot].astype(jnp.float32)
        gather_up_weight = owned_up_weight[local_slot].astype(jnp.float32)
        forward = jnp.einsum("bnd,brd->bnr", rows_b, gather_down_weight)
        backward = jnp.einsum("bnf,brf->bnr", grad_in, gather_up_weight)
        live_mask = (jnp.arange(BLOCK, dtype=jnp.int32)[None, :] < fills[:, None]).astype(jnp.float32)[:, :, None]
        rank_act = lax.optimization_barrier((forward * shrink * live_mask).astype(jnp.bfloat16)).astype(jnp.float32)
        rank_back = lax.optimization_barrier((backward * expand * live_mask).astype(jnp.bfloat16)).astype(jnp.float32)
        grad_a = jnp.einsum("bnr,bnd->brd", rank_back, rows_b) * shrink
        grad_b = jnp.einsum("bnr,bnf->brf", rank_act, grad_in) * expand
        hot = (local_slot[:, None] == jnp.arange(ADAPTERS_PER_DP, dtype=jnp.int32)[None, :]).astype(jnp.float32)
        down_gradient_sum = jnp.einsum("bs,brd->srd", hot, grad_a)
        up_gradient_sum = jnp.einsum("bs,brf->srf", hot, grad_b)
        refreshed_down_weight = (owned_down_weight.astype(jnp.float32) - down_learning_rate * down_gradient_sum).astype(jnp.bfloat16)
        refreshed_up_weight = (owned_up_weight.astype(jnp.float32) - up_learning_rate * up_gradient_sum).astype(jnp.bfloat16)
        return refreshed_down_weight, refreshed_up_weight

    refreshed_down_weight, refreshed_up_weight = lax.map(owner_update, jnp.arange(N_DP, dtype=jnp.int32))
    return dec_delta, refreshed_down_weight.reshape(ADAPTER_COUNT, ADAPTER_RANK, MODEL_WIDTH), refreshed_up_weight.reshape(ADAPTER_COUNT, ADAPTER_RANK, HIDDEN_UNITS)
```

```python
import functools

import jax
import jax.numpy as jnp
from jax import lax
from jax.experimental import pallas as pl
from jax.experimental.pallas import tpu as pltpu
from jax.sharding import PartitionSpec as P

DOWN_RATE = 4.0
UP_RATE = 0.25
DEPTH = 4
CHUNKS = 4
BLOCK = DEPTH * CHUNKS
MESH = pl.DeviceIdType.MESH
F32, BF16, I32 = jnp.float32, jnp.bfloat16, jnp.int32


def nt_dot(a, b):
    return lax.dot_general(a, b, (((1,), (1,)), ((), ())), preferred_element_type=F32)


def tn_dot(a, b):
    return lax.dot_general(a, b, (((0,), (0,)), ((), ())), preferred_element_type=F32)


def nn_dot(a, b):
    return jnp.dot(a, b, preferred_element_type=F32)


def iota(shape, axis):
    return lax.broadcasted_iota(I32, shape, axis)


def kernel(
    geometry,
    dec_index_ref,
    store_ref,
    store_s_ref,
    blk_s_ref,
    live_s_ref,
    dec_hbm,
    rows_hbm,
    grad_hbm,
    down_hbm,
    up_hbm,
    delta_out,
    down_out,
    up_out,
    dec,
    rows,
    grad,
    down,
    up,
    send,
    got,
    meta2,
    meta_send,
    meta_got,
    part,
    part_got,
    lpart,
    lpart_got,
    dsend,
    dgot,
    total,
    load_sems,
    send_sem,
    got_sems,
    meta_send_sem,
    meta_got_sems,
    part_send_sem,
    part_got_sems,
    lpart_send_sem,
    lpart_got_sem,
    dsend_sem,
    dgot_sems,
):
    zs, xs, ts, shrink, expand = geometry
    owners = zs * xs
    wide = 2 * xs
    groups = zs // 2
    gr = wide * BLOCK
    me = lax.axis_index("dp")
    t = lax.axis_index("tensor")
    z, x = me // xs, me % xs
    count = dec.shape[0]
    wc = dec.shape[1] // CHUNKS
    hc = grad.shape[1] // CHUNKS

    def offset(i):
        k = i // wide
        half = (i % wide) // xs
        dz = k + half * (zs - 2 * k - (zs // 2) * ((zs - k) // zs))
        return dz, i % xs

    def owner_of(i):
        dz, dx = offset(i)
        return ((z + dz) % zs) * xs + (x + dx) % xs

    def source_of(i):
        dz, dx = offset(i)
        return ((z + zs - dz) % zs) * xs + (x + xs - dx) % xs

    def load(k, src, dst):
        return pltpu.make_async_copy(src, dst, load_sems.at[k])

    loads = [
        load(0, dec_hbm, dec),
        load(1, rows_hbm, rows),
        load(2, down_hbm, down),
        load(3, grad_hbm, grad),
        load(4, up_hbm, up),
    ]
    for one in loads:
        one.start()

    barrier = pltpu.get_barrier_semaphore()

    def greet(i, carry):
        pl.semaphore_signal(barrier, inc=1, device_id=(owner_of(i), t), device_id_type=MESH)
        return carry

    lax.fori_loop(1, owners, greet, 0)

    def greet_t(j, carry):
        pl.semaphore_signal(barrier, inc=1, device_id=(me, (t + j) % ts), device_id_type=MESH)
        return carry

    lax.fori_loop(1, ts, greet_t, 0)

    adapters = store_ref.shape[1]
    hits = (iota((adapters, count), 0) == dec_index_ref[...]).astype(F32).astype(BF16)
    table = jnp.broadcast_to(store_ref[...], (8, adapters)).astype(F32).astype(BF16)
    slot = nn_dot(table, hits)[0:1].astype(I32)
    owner, local = slot // 2, slot % 2
    dz = (owner // xs - z + zs) % zs
    dx = (owner % xs - x + xs) % xs
    half = (dz >= zs // 2).astype(I32)
    k = jnp.where(dz < zs // 2, dz, jnp.where(dz == zs // 2, 0, zs - dz))
    block = k * wide + half * xs + dx
    square = (count, count)
    block_rows = jnp.broadcast_to(block, square)
    block_cols = jnp.transpose(block_rows.astype(F32)).astype(I32)
    same = jnp.logical_and(block_rows == block_cols, iota(square, 0) < iota(square, 1))
    before = jnp.sum(same.astype(F32), axis=0, keepdims=True).astype(I32)
    place = block * BLOCK + before
    code = jnp.broadcast_to(place * 2 + local, square)
    code_cols = jnp.transpose(code.astype(F32)).astype(I32)
    place_cols = code_cols // 2
    named = (code_cols % 2 + 1).astype(F32)
    lanes = iota((count, 128), 1)
    slot_cols = jnp.broadcast_to(place_cols[:, 0:1] % BLOCK, (count, 128))
    spread = jnp.where(
        lanes % DEPTH == slot_cols, jnp.broadcast_to(named[:, 0:1], (count, 128)), 0.0
    )
    in_block = (iota((owners, count), 0) == block).astype(F32).astype(BF16)
    meta2[...] = nn_dot(in_block, spread.astype(BF16))

    def lift(i, carry):
        meta_send[i] = meta2[pl.ds(i, 1), :]
        return carry

    lax.fori_loop(0, owners, lift, 0)
    meta_got[0] = meta2[0:1, :]

    loads[0].wait()
    pl.semaphore_wait(barrier, owners - 1 + ts - 1)

    def row_copy(i):
        at = pl.ds(pl.multiple_of(i * BLOCK, BLOCK), BLOCK)
        return pltpu.make_async_remote_copy(
            src_ref=send.at[at],
            dst_ref=got.at[at],
            send_sem=send_sem,
            recv_sem=got_sems.at[i // wide],
            device_id=(owner_of(i), t),
            device_id_type=MESH,
        )

    def meta_copy(i):
        return pltpu.make_async_remote_copy(
            src_ref=meta_send.at[i],
            dst_ref=meta_got.at[i],
            send_sem=meta_send_sem,
            recv_sem=meta_got_sems.at[i // wide],
            device_id=(owner_of(i), t),
            device_id_type=MESH,
        )

    def start_rows(i, carry):
        meta_copy(i).start()
        row_copy(i).start()
        return carry

    def dispatch(g):
        base = pl.multiple_of(g * gr, gr)
        rel = iota((gr, count), 0) + base
        sum_rows = jnp.zeros((gr, wc), F32)
        for c in range(CHUNKS):
            chosen = (rel == place + c * DEPTH).astype(F32).astype(BF16)
            sum_rows += nn_dot(chosen, dec[:, c * wc : (c + 1) * wc])
        send[pl.ds(base, gr), :] = sum_rows.astype(BF16)

    dispatch(0)
    lax.fori_loop(1, wide, start_rows, 0)
    got[0:BLOCK, :] = send[0:BLOCK, :]

    def dispatch_more(g, carry):
        dispatch(g)
        lax.fori_loop(g * wide, (g + 1) * wide, start_rows, 0)
        return carry

    lax.fori_loop(1, groups, dispatch_more, 0)

    rank = down.shape[0] // 2
    learn = rows.shape[0]
    own_slot = store_s_ref[blk_s_ref[0]] % 2
    aj = iota((learn, 2 * rank), 1)
    own = (aj // rank == own_slot).astype(F32)
    loads[1].wait()
    loads[2].wait()
    forward = nt_dot(rows[...], down[...]) * own
    loads[3].wait()
    loads[4].wait()
    backward = nt_dot(grad[...], up[...]) * own
    forward = forward + pltpu.roll(forward, rank, 1)
    backward = backward + pltpu.roll(backward, rank, 1)
    lpart[...] = jnp.where(aj < rank, forward, backward)

    def lpart_copy(j):
        return pltpu.make_async_remote_copy(
            src_ref=lpart,
            dst_ref=lpart_got.at[j - 1],
            send_sem=lpart_send_sem,
            recv_sem=lpart_got_sem,
            device_id=(me, (t + j) % ts),
            device_id_type=MESH,
        )

    def start_lpart(j, carry):
        lpart_copy(j).start()
        return carry

    lax.fori_loop(1, ts, start_lpart, 0)

    def wait_group(g, ref, size, sems):
        @pl.when(g == 0)
        def _():
            view = ref.at[pl.ds(size, (wide - 1) * size)]
            pltpu.make_async_copy(view, view, sems.at[g]).wait()

        @pl.when(g > 0)
        def _():
            view = ref.at[pl.ds(pl.multiple_of(g * wide * size, wide * size), wide * size)]
            pltpu.make_async_copy(view, view, sems.at[g]).wait()

    chunk_of = (iota((gr, 2 * rank), 0) % BLOCK) // DEPTH
    lane = iota((gr, 2 * rank), 1)

    def chosen_mask(g):
        ids = meta_got[pl.ds(g * wide, wide)]
        ids = jnp.broadcast_to(ids, (wide, BLOCK, 128)).reshape(gr, 128)
        mine = iota((gr, 128), 1) == iota((gr, 128), 0) % DEPTH
        which = jnp.sum(jnp.where(mine, ids, 0.0), axis=1, keepdims=True)
        return (which == (lane // rank + 1).astype(F32)).astype(F32)

    pairs = wide // 2
    top3 = iota((wide, 8, 2 * rank), 1) < DEPTH
    left3 = iota((wide, 8, 2 * rank), 2) < rank

    def part_copy(g, j):
        return pltpu.make_async_remote_copy(
            src_ref=part.at[g],
            dst_ref=part_got.at[g, j - 1],
            send_sem=part_send_sem,
            recv_sem=part_got_sems.at[g],
            device_id=(me, (t + j) % ts),
            device_id_type=MESH,
        )

    def ranks(g):
        wait_group(g, got, BLOCK, got_sems)
        wait_group(g, meta_got, 1, meta_got_sems)
        at = pl.ds(pl.multiple_of(g * gr, gr), gr)
        block_rows = got[at, :]
        both = jnp.zeros((gr, 2 * rank), F32)
        for c in range(CHUNKS):
            one = nt_dot(block_rows, down[:, c * wc : (c + 1) * wc])
            both = both + jnp.where(chunk_of == c, one, 0.0)
        both = both * chosen_mask(g)
        both = both.reshape(wide, 2, 8, 2 * rank)
        both = both[:, 0] + both[:, 1]
        both = both + pltpu.roll(both, DEPTH, 1)
        both = both + pltpu.roll(both, rank, 2)
        both = both.reshape(2, pairs, 8, 2 * rank)
        two = jnp.where(top3[:pairs], both[0], both[1])
        two = two.reshape(2, pairs // 2, 8, 2 * rank)
        part[g] = jnp.where(left3[: pairs // 2], two[0], two[1])

        def start(j, carry):
            part_copy(g, j).start()
            return carry

        lax.fori_loop(1, ts, start, 0)

    def delta_copy(i):
        at = pl.ds(pl.multiple_of(i * BLOCK, BLOCK), BLOCK)
        return pltpu.make_async_remote_copy(
            src_ref=dsend.at[at],
            dst_ref=dgot.at[at],
            send_sem=dsend_sem,
            recv_sem=dgot_sems.at[i // wide],
            device_id=(source_of(i), t),
            device_id_type=MESH,
        )

    def start_delta(i, carry):
        delta_copy(i).start()
        return carry

    def deltas(g):
        view = part_got.at[g]
        pltpu.make_async_copy(view, view, part_got_sems.at[g]).wait()
        v = part[g]
        for j in range(ts - 1):
            v = v + part_got[g, j]
        v = (v * shrink).astype(BF16).astype(F32)
        turned = pltpu.roll(v, rank, 2)
        keep = left3[: pairs // 2]
        two = jnp.concatenate([jnp.where(keep, v, turned), jnp.where(keep, turned, v)], axis=0)
        turned = pltpu.roll(two, DEPTH, 1)
        keep = top3[:pairs]
        both = jnp.concatenate([jnp.where(keep, two, turned), jnp.where(keep, turned, two)], axis=0)
        both = jnp.broadcast_to(both[:, None], (wide, 2, 8, 2 * rank)).reshape(gr, 2 * rank)
        both = both * chosen_mask(g)
        base = pl.multiple_of(g * gr, gr)
        sum_rows = jnp.zeros((gr, hc), F32)
        for c in range(CHUNKS):
            left = jnp.where(chunk_of == c, both, 0.0).astype(BF16)
            sum_rows += nn_dot(left, up[:, c * hc : (c + 1) * hc])
        dsend[pl.ds(base, gr), :] = (sum_rows * expand).astype(BF16)

        @pl.when(g == 0)
        def _():
            dgot[0:BLOCK, :] = dsend[0:BLOCK, :]
            lax.fori_loop(1, wide, start_delta, 0)

        @pl.when(g > 0)
        def _():
            lax.fori_loop(g * wide, (g + 1) * wide, start_delta, 0)

    ranks(0)

    def step(g, carry):
        ranks(g)
        deltas(g - 1)
        return carry

    lax.fori_loop(1, groups, step, 0)
    deltas(groups - 1)

    pltpu.make_async_copy(lpart_got, lpart_got, lpart_got_sem).wait()
    v = lpart[...]
    for j in range(ts - 1):
        v = v + lpart_got[j]
    live = (iota((learn, 2 * rank), 0) < live_s_ref[0]).astype(F32)
    scale = jnp.where(aj < rank, shrink, expand)
    v = (v * scale * live).astype(BF16).astype(F32)
    turned = pltpu.roll(v, rank, 1)
    act = (jnp.where(aj < rank, v, turned) * own).astype(BF16)
    back = (jnp.where(aj < rank, turned, v) * own).astype(BF16)
    for c in range(CHUNKS):
        at = slice(c * wc, (c + 1) * wc)
        g_a = tn_dot(back, rows[:, at]) * shrink
        down_out[:, at] = (down[:, at].astype(F32) - DOWN_RATE * g_a).astype(BF16)
    for c in range(CHUNKS):
        at = slice(c * hc, (c + 1) * hc)
        g_b = tn_dot(act, grad[:, at]) * expand
        up_out[:, at] = (up[:, at].astype(F32) - UP_RATE * g_b).astype(BF16)

    total[...] = jnp.zeros_like(total)
    place_128 = jnp.broadcast_to(place_cols[:, 0:1], (count, gr))

    def combine(g, carry):
        wait_group(g, dgot, BLOCK, dgot_sems)
        base = pl.multiple_of(g * gr, gr)
        rel = iota((count, gr), 1) + base
        arrived = dgot[pl.ds(base, gr), :]
        for c in range(CHUNKS):
            chosen = (rel == place_128 + c * DEPTH).astype(F32).astype(BF16)
            total[:, c * hc : (c + 1) * hc] += nn_dot(chosen, arrived)
        return carry

    lax.fori_loop(0, groups, combine, 0)
    delta_out[...] = total[...].astype(BF16)

    def drain(view, sem):
        pltpu.make_async_copy(view, view, sem).wait()

    drain(send.at[pl.ds(BLOCK, (owners - 1) * BLOCK)], send_sem)
    drain(meta_send.at[pl.ds(1, owners - 1)], meta_send_sem)
    drain(dsend.at[pl.ds(BLOCK, (owners - 1) * BLOCK)], dsend_sem)
    drain(lpart_got, lpart_send_sem)
    drain(part_got, part_send_sem)


def local(
    decode_input_rows,
    decode_adapter_index,
    adapter_storage_index,
    learner_input_rows,
    learner_gradient,
    block_adapter_index,
    block_live_count,
    adapter_down_weight,
    adapter_up_weight,
):
    owners = lax.axis_size("dp")
    ts = lax.axis_size("tensor")
    xs = 4
    zs = owners // xs
    held, rank, width = adapter_down_weight.shape
    hidden = adapter_up_weight.shape[2]
    count = decode_input_rows.shape[0]
    learn = learner_input_rows.shape[0]
    shrink = (width * ts) ** (-0.5)
    expand = rank ** (-0.5)
    groups = zs // 2
    wide = 2 * xs
    vmem = pl.BlockSpec(memory_space=pltpu.VMEM)
    smem = pl.BlockSpec(memory_space=pltpu.SMEM)
    hbm = pl.BlockSpec(memory_space=pl.ANY)
    dma = pltpu.SemaphoreType.DMA
    packed = (wide // 4, 8, 2 * rank)
    delta, down, up = pl.pallas_call(
        functools.partial(kernel, (zs, xs, ts, shrink, expand)),
        out_shape=(
            jax.ShapeDtypeStruct((count, hidden), BF16),
            jax.ShapeDtypeStruct((held * rank, width), BF16),
            jax.ShapeDtypeStruct((held * rank, hidden), BF16),
        ),
        in_specs=[vmem, vmem, smem, smem, smem, hbm, hbm, hbm, hbm, hbm],
        out_specs=(vmem, vmem, vmem),
        scratch_shapes=[
            pltpu.VMEM((count, width), BF16),
            pltpu.VMEM((learn, width), BF16),
            pltpu.VMEM((learn, hidden), BF16),
            pltpu.VMEM((held * rank, width), BF16),
            pltpu.VMEM((held * rank, hidden), BF16),
            pltpu.VMEM((owners * BLOCK, width // CHUNKS), BF16),
            pltpu.VMEM((owners * BLOCK, width // CHUNKS), BF16),
            pltpu.VMEM((owners, 128), F32),
            pltpu.VMEM((owners, 1, 128), F32),
            pltpu.VMEM((owners, 1, 128), F32),
            pltpu.VMEM((groups,) + packed, F32),
            pltpu.VMEM((groups, ts - 1) + packed, F32),
            pltpu.VMEM((learn, 2 * rank), F32),
            pltpu.VMEM((ts - 1, learn, 2 * rank), F32),
            pltpu.VMEM((owners * BLOCK, hidden // CHUNKS), BF16),
            pltpu.VMEM((owners * BLOCK, hidden // CHUNKS), BF16),
            pltpu.VMEM((count, hidden), F32),
            dma((5,)),
            dma,
            dma((groups,)),
            dma,
            dma((groups,)),
            dma,
            dma((groups,)),
            dma,
            dma,
            dma,
            dma((groups,)),
        ],
        compiler_params=pltpu.CompilerParams(
            collective_id=0, has_side_effects=True, vmem_limit_bytes=48 * 1024 * 1024
        ),
    )(
        decode_adapter_index.reshape(1, count),
        adapter_storage_index.reshape(1, -1),
        adapter_storage_index,
        block_adapter_index,
        block_live_count,
        decode_input_rows,
        learner_input_rows,
        learner_gradient,
        adapter_down_weight.reshape(held * rank, width),
        adapter_up_weight.reshape(held * rank, hidden),
    )
    return delta, down.reshape(held, rank, width), up.reshape(held, rank, hidden)


def solution(mesh):
    in_specs = (
        P("dp", "tensor"),
        P("dp"),
        P(),
        P("dp", "tensor"),
        P("dp", "tensor"),
        P("dp"),
        P("dp"),
        P("dp", None, "tensor"),
        P("dp", None, "tensor"),
    )
    out_specs = (P("dp", "tensor"), P("dp", None, "tensor"), P("dp", None, "tensor"))
    return jax.shard_map(local, mesh=mesh, in_specs=in_specs, out_specs=out_specs, check_vma=False)
```

```python
import functools

import jax
import jax.numpy as jnp
from jax import lax
from jax.experimental import pallas as pl
from jax.experimental.pallas import tpu as pltpu
from jax.sharding import PartitionSpec as P

DOWN_RATE = 4.0
UP_RATE = 0.25
DEPTH = 4
CHUNKS = 4
BLOCK = DEPTH * CHUNKS
MESH = pl.DeviceIdType.MESH
F32, BF16, I32 = jnp.float32, jnp.bfloat16, jnp.int32


def nt_dot(a, b):
    return lax.dot_general(a, b, (((1,), (1,)), ((), ())), preferred_element_type=F32)


def tn_dot(a, b):
    return lax.dot_general(a, b, (((0,), (0,)), ((), ())), preferred_element_type=F32)


def nn_dot(a, b):
    return jnp.dot(a, b, preferred_element_type=F32)


def iota(shape, axis):
    return lax.broadcasted_iota(I32, shape, axis)


def kernel(
    geometry,
    dec_index_hbm,
    store_hbm,
    store_flat_hbm,
    blk_hbm,
    live_hbm,
    dec_hbm,
    rows_hbm,
    grad_hbm,
    down_hbm,
    up_hbm,
    delta_out,
    down_out,
    up_out,
    dec_index_ref,
    store_ref,
    store_s_ref,
    blk_s_ref,
    live_s_ref,
    dec,
    rows,
    grad,
    down,
    up,
    send,
    got,
    meta2,
    meta_send,
    meta_got,
    part,
    part_got,
    lpart,
    lpart_got,
    dsend,
    dgot,
    total,
    load_sems,
    send_sem,
    got_sems,
    meta_send_sem,
    meta_got_sems,
    part_send_sem,
    part_got_sems,
    lpart_send_sem,
    lpart_got_sem,
    dsend_sem,
    dgot_sems,
):
    zs, xs, ts, shrink, expand = geometry
    owners = zs * xs
    wide = 2 * xs
    groups = zs // 2
    gr = wide * BLOCK
    me = lax.axis_index("dp")
    t = lax.axis_index("tensor")
    z, x = me // xs, me % xs
    count = dec.shape[0]
    wc = dec.shape[1] // CHUNKS
    hc = grad.shape[1] // CHUNKS

    def offset(i):
        k = i // wide
        half = (i % wide) // xs
        dz = k + half * (zs - 2 * k - (zs // 2) * ((zs - k) // zs))
        return dz, i % xs

    def owner_of(i):
        dz, dx = offset(i)
        return ((z + dz) % zs) * xs + (x + dx) % xs

    def source_of(i):
        dz, dx = offset(i)
        return ((z + zs - dz) % zs) * xs + (x + xs - dx) % xs

    def load(k, src, dst):
        return pltpu.make_async_copy(src, dst, load_sems.at[k])

    loads = [
        load(0, dec_hbm, dec),
        load(1, rows_hbm, rows),
        load(2, down_hbm, down),
        load(3, grad_hbm, grad),
        load(4, up_hbm, up),
        load(5, dec_index_hbm, dec_index_ref),
        load(6, store_hbm, store_ref),
        load(7, store_flat_hbm, store_s_ref),
        load(8, blk_hbm, blk_s_ref),
        load(9, live_hbm, live_s_ref),
    ]
    loads = loads[:1] + loads[5:] + loads[1:5]
    for one in loads:
        one.start()

    barrier = pltpu.get_barrier_semaphore()

    def greet(i, carry):
        pl.semaphore_signal(barrier, inc=1, device_id=(owner_of(i), t), device_id_type=MESH)
        return carry

    lax.fori_loop(1, owners, greet, 0)

    def greet_t(j, carry):
        pl.semaphore_signal(barrier, inc=1, device_id=(me, (t + j) % ts), device_id_type=MESH)
        return carry

    lax.fori_loop(1, ts, greet_t, 0)

    for one in loads[1:6]:
        one.wait()

    adapters = store_ref.shape[1]
    hits = (iota((adapters, count), 0) == dec_index_ref[...]).astype(F32).astype(BF16)
    table = jnp.broadcast_to(store_ref[...], (8, adapters)).astype(F32).astype(BF16)
    slot = nn_dot(table, hits)[0:1].astype(I32)
    owner, local = slot // 2, slot % 2
    dz = (owner // xs - z + zs) % zs
    dx = (owner % xs - x + xs) % xs
    half = (dz >= zs // 2).astype(I32)
    k = jnp.where(dz < zs // 2, dz, jnp.where(dz == zs // 2, 0, zs - dz))
    block = k * wide + half * xs + dx
    square = (count, count)
    block_rows = jnp.broadcast_to(block, square)
    block_cols = jnp.transpose(block_rows.astype(F32)).astype(I32)
    same = jnp.logical_and(block_rows == block_cols, iota(square, 0) < iota(square, 1))
    before = jnp.sum(same.astype(F32), axis=0, keepdims=True).astype(I32)
    place = block * BLOCK + before
    code = jnp.broadcast_to(place * 2 + local, square)
    code_cols = jnp.transpose(code.astype(F32)).astype(I32)
    place_cols = code_cols // 2
    named = (code_cols % 2 + 1).astype(F32)
    lanes = iota((count, 128), 1)
    slot_cols = jnp.broadcast_to(place_cols[:, 0:1] % BLOCK, (count, 128))
    spread = jnp.where(
        lanes % DEPTH == slot_cols, jnp.broadcast_to(named[:, 0:1], (count, 128)), 0.0
    )
    in_block = (iota((owners, count), 0) == block).astype(F32).astype(BF16)
    meta2[...] = nn_dot(in_block, spread.astype(BF16))

    def lift(i, carry):
        meta_send[i] = meta2[pl.ds(i, 1), :]
        return carry

    lax.fori_loop(0, owners, lift, 0)
    meta_got[0] = meta2[0:1, :]

    loads[0].wait()
    pl.semaphore_wait(barrier, owners - 1 + ts - 1)

    def row_copy(i):
        at = pl.ds(pl.multiple_of(i * BLOCK, BLOCK), BLOCK)
        return pltpu.make_async_remote_copy(
            src_ref=send.at[at],
            dst_ref=got.at[at],
            send_sem=send_sem,
            recv_sem=got_sems.at[i // wide],
            device_id=(owner_of(i), t),
            device_id_type=MESH,
        )

    def meta_copy(i):
        return pltpu.make_async_remote_copy(
            src_ref=meta_send.at[i],
            dst_ref=meta_got.at[i],
            send_sem=meta_send_sem,
            recv_sem=meta_got_sems.at[i // wide],
            device_id=(owner_of(i), t),
            device_id_type=MESH,
        )

    def start_rows(i, carry):
        meta_copy(i).start()
        row_copy(i).start()
        return carry

    def dispatch(g):
        base = pl.multiple_of(g * gr, gr)
        rel = iota((gr, count), 0) + base
        sum_rows = jnp.zeros((gr, wc), F32)
        for c in range(CHUNKS):
            chosen = (rel == place + c * DEPTH).astype(F32).astype(BF16)
            sum_rows += nn_dot(chosen, dec[:, c * wc : (c + 1) * wc])
        send[pl.ds(base, gr), :] = sum_rows.astype(BF16)

    dispatch(0)
    lax.fori_loop(1, wide, start_rows, 0)
    got[0:BLOCK, :] = send[0:BLOCK, :]

    def dispatch_more(g, carry):
        dispatch(g)
        lax.fori_loop(g * wide, (g + 1) * wide, start_rows, 0)
        return carry

    lax.fori_loop(1, groups, dispatch_more, 0)

    rank = down.shape[0] // 2
    learn = rows.shape[0]
    own_slot = store_s_ref[blk_s_ref[0]] % 2
    aj = iota((learn, 2 * rank), 1)
    own = (aj // rank == own_slot).astype(F32)
    loads[6].wait()
    loads[7].wait()
    forward = nt_dot(rows[...], down[...]) * own
    loads[8].wait()
    loads[9].wait()
    backward = nt_dot(grad[...], up[...]) * own
    forward = forward + pltpu.roll(forward, rank, 1)
    backward = backward + pltpu.roll(backward, rank, 1)
    lpart[...] = jnp.where(aj < rank, forward, backward)

    def lpart_copy(j):
        return pltpu.make_async_remote_copy(
            src_ref=lpart,
            dst_ref=lpart_got.at[j - 1],
            send_sem=lpart_send_sem,
            recv_sem=lpart_got_sem,
            device_id=(me, (t + j) % ts),
            device_id_type=MESH,
        )

    def start_lpart(j, carry):
        lpart_copy(j).start()
        return carry

    lax.fori_loop(1, ts, start_lpart, 0)

    def wait_group(g, ref, size, sems):
        @pl.when(g == 0)
        def _():
            view = ref.at[pl.ds(size, (wide - 1) * size)]
            pltpu.make_async_copy(view, view, sems.at[g]).wait()

        @pl.when(g > 0)
        def _():
            view = ref.at[pl.ds(pl.multiple_of(g * wide * size, wide * size), wide * size)]
            pltpu.make_async_copy(view, view, sems.at[g]).wait()

    chunk_of = (iota((gr, 2 * rank), 0) % BLOCK) // DEPTH
    lane = iota((gr, 2 * rank), 1)

    def chosen_mask(g):
        ids = meta_got[pl.ds(g * wide, wide)]
        ids = jnp.broadcast_to(ids, (wide, BLOCK, 128)).reshape(gr, 128)
        mine = iota((gr, 128), 1) == iota((gr, 128), 0) % DEPTH
        which = jnp.sum(jnp.where(mine, ids, 0.0), axis=1, keepdims=True)
        return (which == (lane // rank + 1).astype(F32)).astype(F32)

    pairs = wide // 2
    top3 = iota((wide, 8, 2 * rank), 1) < DEPTH
    left3 = iota((wide, 8, 2 * rank), 2) < rank

    def part_copy(g, j):
        return pltpu.make_async_remote_copy(
            src_ref=part.at[g],
            dst_ref=part_got.at[g, j - 1],
            send_sem=part_send_sem,
            recv_sem=part_got_sems.at[g],
            device_id=(me, (t + j) % ts),
            device_id_type=MESH,
        )

    def ranks(g):
        wait_group(g, got, BLOCK, got_sems)
        wait_group(g, meta_got, 1, meta_got_sems)
        at = pl.ds(pl.multiple_of(g * gr, gr), gr)
        block_rows = got[at, :]
        both = jnp.zeros((gr, 2 * rank), F32)
        for c in range(CHUNKS):
            one = nt_dot(block_rows, down[:, c * wc : (c + 1) * wc])
            both = both + jnp.where(chunk_of == c, one, 0.0)
        both = both * chosen_mask(g)
        both = both.reshape(wide, 2, 8, 2 * rank)
        both = both[:, 0] + both[:, 1]
        both = both + pltpu.roll(both, DEPTH, 1)
        both = both + pltpu.roll(both, rank, 2)
        both = both.reshape(2, pairs, 8, 2 * rank)
        two = jnp.where(top3[:pairs], both[0], both[1])
        two = two.reshape(2, pairs // 2, 8, 2 * rank)
        part[g] = jnp.where(left3[: pairs // 2], two[0], two[1])

        def start(j, carry):
            part_copy(g, j).start()
            return carry

        lax.fori_loop(1, ts, start, 0)

    def delta_copy(i):
        at = pl.ds(pl.multiple_of(i * BLOCK, BLOCK), BLOCK)
        return pltpu.make_async_remote_copy(
            src_ref=dsend.at[at],
            dst_ref=dgot.at[at],
            send_sem=dsend_sem,
            recv_sem=dgot_sems.at[i // wide],
            device_id=(source_of(i), t),
            device_id_type=MESH,
        )

    def start_delta(i, carry):
        delta_copy(i).start()
        return carry

    def deltas(g):
        view = part_got.at[g]
        pltpu.make_async_copy(view, view, part_got_sems.at[g]).wait()
        v = part[g]
        for j in range(ts - 1):
            v = v + part_got[g, j]
        v = (v * shrink).astype(BF16).astype(F32)
        turned = pltpu.roll(v, rank, 2)
        keep = left3[: pairs // 2]
        two = jnp.concatenate([jnp.where(keep, v, turned), jnp.where(keep, turned, v)], axis=0)
        turned = pltpu.roll(two, DEPTH, 1)
        keep = top3[:pairs]
        both = jnp.concatenate([jnp.where(keep, two, turned), jnp.where(keep, turned, two)], axis=0)
        both = jnp.broadcast_to(both[:, None], (wide, 2, 8, 2 * rank)).reshape(gr, 2 * rank)
        both = both * chosen_mask(g)
        base = pl.multiple_of(g * gr, gr)
        sum_rows = jnp.zeros((gr, hc), F32)
        for c in range(CHUNKS):
            left = jnp.where(chunk_of == c, both, 0.0).astype(BF16)
            sum_rows += nn_dot(left, up[:, c * hc : (c + 1) * hc])
        dsend[pl.ds(base, gr), :] = (sum_rows * expand).astype(BF16)

        @pl.when(g == 0)
        def _():
            dgot[0:BLOCK, :] = dsend[0:BLOCK, :]
            lax.fori_loop(1, wide, start_delta, 0)

        @pl.when(g > 0)
        def _():
            lax.fori_loop(g * wide, (g + 1) * wide, start_delta, 0)

    ranks(0)

    def step(g, carry):
        ranks(g)
        deltas(g - 1)
        return carry

    lax.fori_loop(1, groups, step, 0)
    deltas(groups - 1)

    pltpu.make_async_copy(lpart_got, lpart_got, lpart_got_sem).wait()
    v = lpart[...]
    for j in range(ts - 1):
        v = v + lpart_got[j]
    live = (iota((learn, 2 * rank), 0) < live_s_ref[0]).astype(F32)
    scale = jnp.where(aj < rank, shrink, expand)
    v = (v * scale * live).astype(BF16).astype(F32)
    turned = pltpu.roll(v, rank, 1)
    act = (jnp.where(aj < rank, v, turned) * own).astype(BF16)
    back = (jnp.where(aj < rank, turned, v) * own).astype(BF16)
    for c in range(CHUNKS):
        at = slice(c * wc, (c + 1) * wc)
        g_a = tn_dot(back, rows[:, at]) * shrink
        down_out[:, at] = (down[:, at].astype(F32) - DOWN_RATE * g_a).astype(BF16)
    for c in range(CHUNKS):
        at = slice(c * hc, (c + 1) * hc)
        g_b = tn_dot(act, grad[:, at]) * expand
        up_out[:, at] = (up[:, at].astype(F32) - UP_RATE * g_b).astype(BF16)

    total[...] = jnp.zeros_like(total)
    place_128 = jnp.broadcast_to(place_cols[:, 0:1], (count, gr))

    def combine(g, carry):
        wait_group(g, dgot, BLOCK, dgot_sems)
        base = pl.multiple_of(g * gr, gr)
        rel = iota((count, gr), 1) + base
        arrived = dgot[pl.ds(base, gr), :]
        for c in range(CHUNKS):
            chosen = (rel == place_128 + c * DEPTH).astype(F32).astype(BF16)
            total[:, c * hc : (c + 1) * hc] += nn_dot(chosen, arrived)
        return carry

    lax.fori_loop(0, groups, combine, 0)
    delta_out[...] = total[...].astype(BF16)

    def drain(view, sem):
        pltpu.make_async_copy(view, view, sem).wait()

    drain(send.at[pl.ds(BLOCK, (owners - 1) * BLOCK)], send_sem)
    drain(meta_send.at[pl.ds(1, owners - 1)], meta_send_sem)
    drain(dsend.at[pl.ds(BLOCK, (owners - 1) * BLOCK)], dsend_sem)
    drain(lpart_got, lpart_send_sem)
    drain(part_got, part_send_sem)


def local(
    decode_input_rows,
    decode_adapter_index,
    adapter_storage_index,
    learner_input_rows,
    learner_gradient,
    block_adapter_index,
    block_live_count,
    adapter_down_weight,
    adapter_up_weight,
):
    owners = lax.axis_size("dp")
    ts = lax.axis_size("tensor")
    xs = 4
    zs = owners // xs
    held, rank, width = adapter_down_weight.shape
    hidden = adapter_up_weight.shape[2]
    count = decode_input_rows.shape[0]
    learn = learner_input_rows.shape[0]
    shrink = (width * ts) ** (-0.5)
    expand = rank ** (-0.5)
    groups = zs // 2
    wide = 2 * xs
    vmem = pl.BlockSpec(memory_space=pltpu.VMEM)
    hbm = pl.BlockSpec(memory_space=pltpu.HBM)
    dma = pltpu.SemaphoreType.DMA
    packed = (wide // 4, 8, 2 * rank)
    delta, down, up = pl.pallas_call(
        functools.partial(kernel, (zs, xs, ts, shrink, expand)),
        out_shape=(
            jax.ShapeDtypeStruct((count, hidden), BF16),
            jax.ShapeDtypeStruct((held * rank, width), BF16),
            jax.ShapeDtypeStruct((held * rank, hidden), BF16),
        ),
        in_specs=[hbm] * 10,
        out_specs=(vmem, vmem, vmem),
        scratch_shapes=[
            pltpu.VMEM((1, count), I32),
            pltpu.VMEM((1, adapter_storage_index.shape[0]), I32),
            pltpu.SMEM((adapter_storage_index.shape[0],), I32),
            pltpu.SMEM((1,), I32),
            pltpu.SMEM((1,), I32),
            pltpu.VMEM((count, width), BF16),
            pltpu.VMEM((learn, width), BF16),
            pltpu.VMEM((learn, hidden), BF16),
            pltpu.VMEM((held * rank, width), BF16),
            pltpu.VMEM((held * rank, hidden), BF16),
            pltpu.VMEM((owners * BLOCK, width // CHUNKS), BF16),
            pltpu.VMEM((owners * BLOCK, width // CHUNKS), BF16),
            pltpu.VMEM((owners, 128), F32),
            pltpu.VMEM((owners, 1, 128), F32),
            pltpu.VMEM((owners, 1, 128), F32),
            pltpu.VMEM((groups,) + packed, F32),
            pltpu.VMEM((groups, ts - 1) + packed, F32),
            pltpu.VMEM((learn, 2 * rank), F32),
            pltpu.VMEM((ts - 1, learn, 2 * rank), F32),
            pltpu.VMEM((owners * BLOCK, hidden // CHUNKS), BF16),
            pltpu.VMEM((owners * BLOCK, hidden // CHUNKS), BF16),
            pltpu.VMEM((count, hidden), F32),
            dma((10,)),
            dma,
            dma((groups,)),
            dma,
            dma((groups,)),
            dma,
            dma((groups,)),
            dma,
            dma,
            dma,
            dma((groups,)),
        ],
        compiler_params=pltpu.CompilerParams(
            collective_id=0, has_side_effects=True, vmem_limit_bytes=58 * 1024 * 1024
        ),
    )(
        decode_adapter_index.reshape(1, count),
        adapter_storage_index.reshape(1, -1),
        adapter_storage_index,
        block_adapter_index,
        block_live_count,
        decode_input_rows,
        learner_input_rows,
        learner_gradient,
        adapter_down_weight.reshape(held * rank, width),
        adapter_up_weight.reshape(held * rank, hidden),
    )
    return delta, down.reshape(held, rank, width), up.reshape(held, rank, hidden)


def solution(mesh):
    in_specs = (
        P("dp", "tensor"),
        P("dp"),
        P(),
        P("dp", "tensor"),
        P("dp", "tensor"),
        P("dp"),
        P("dp"),
        P("dp", None, "tensor"),
        P("dp", None, "tensor"),
    )
    out_specs = (P("dp", "tensor"), P("dp", None, "tensor"), P("dp", None, "tensor"))
    return jax.shard_map(local, mesh=mesh, in_specs=in_specs, out_specs=out_specs, check_vma=False)
```

```python
import functools

import jax
import jax.numpy as jnp
from jax import lax
from jax.experimental import pallas as pl
from jax.experimental.pallas import tpu as pltpu
from jax.sharding import PartitionSpec as P

DOWN_RATE = 4.0
UP_RATE = 0.25
DEPTH = 4
CHUNKS = 4
BLOCK = DEPTH * CHUNKS
KEPT = 12
SPARE = 8
MOVES = ((1, 11), (-1, 10), (-1, 11), (1, 10), (1, 9), (-1, 8))
MESH = pl.DeviceIdType.MESH
F32, BF16, I32 = jnp.float32, jnp.bfloat16, jnp.int32


def nt_dot(a, b):
    return lax.dot_general(a, b, (((1,), (1,)), ((), ())), preferred_element_type=F32)


def tn_dot(a, b):
    return lax.dot_general(a, b, (((0,), (0,)), ((), ())), preferred_element_type=F32)


def nn_dot(a, b):
    return jnp.dot(a, b, preferred_element_type=F32)


def iota(shape, axis):
    return lax.broadcasted_iota(I32, shape, axis)


def kernel(
    geometry,
    dec_index_hbm,
    store_hbm,
    store_flat_hbm,
    blk_hbm,
    live_hbm,
    dec_hbm,
    rows_hbm,
    grad_hbm,
    down_hbm,
    up_hbm,
    delta_out,
    down_out,
    up_out,
    flag_out,
    dec_index_ref,
    store_ref,
    store_s_ref,
    blk_s_ref,
    live_s_ref,
    dec,
    rows,
    grad,
    down,
    up,
    send,
    got,
    meta2,
    meta_send,
    meta_got,
    part,
    part_got,
    lpart,
    lpart_got,
    dsend,
    xgot,
    rmeta2,
    rmeta_send,
    rmeta_got,
    t_slot,
    t_plus,
    t_minus,
    t_in,
    asend,
    agot,
    bsend,
    bgot,
    spill,
    fsend,
    fgot,
    flag_send,
    flag_got,
    flagx_send,
    flagx_got,
    total,
    load_sems,
    send_sem,
    got_sems,
    meta_send_sem,
    meta_got_sems,
    part_send_sem,
    part_got_sems,
    lpart_send_sem,
    lpart_got_sem,
    xsend_sem,
    xgot_sems,
    rmeta_send_sem,
    rmeta_got_sem,
    asend_sem,
    agot_sems,
    bsend_sem,
    bgot_sems,
    fsend_sem,
    fgot_sem,
    flag_sems,
):
    zs, xs, ts, shrink, expand = geometry
    owners = zs * xs
    wide = 2 * xs
    groups = zs // 2
    gr = wide * BLOCK
    me = lax.axis_index("dp")
    t = lax.axis_index("tensor")
    z, x = me // xs, me % xs
    count = dec.shape[0]
    wc = dec.shape[1] // CHUNKS
    hc = grad.shape[1] // CHUNKS

    def offset(i):
        k = i // wide
        half = (i % wide) // xs
        dz = k + half * (zs - 2 * k - (zs // 2) * ((zs - k) // zs))
        return dz, i % xs

    def owner_of(i):
        dz, dx = offset(i)
        return ((z + dz) % zs) * xs + (x + dx) % xs

    def x_peer(dx):
        return z * xs + (x + dx) % xs

    def z_peer(dz):
        return ((z + dz) % zs) * xs + x

    def flow_step(f):
        return offset(f * xs)[0]

    def load(k, src, dst):
        return pltpu.make_async_copy(src, dst, load_sems.at[k])

    loads = [
        load(0, dec_hbm, dec),
        load(1, rows_hbm, rows),
        load(2, down_hbm, down),
        load(3, grad_hbm, grad),
        load(4, up_hbm, up),
        load(5, dec_index_hbm, dec_index_ref),
        load(6, store_hbm, store_ref),
        load(7, store_flat_hbm, store_s_ref),
        load(8, blk_hbm, blk_s_ref),
        load(9, live_hbm, live_s_ref),
    ]
    loads = loads[:1] + loads[5:] + loads[1:5]
    for one in loads:
        one.start()

    barrier = pltpu.get_barrier_semaphore()

    def greet(i, carry):
        pl.semaphore_signal(barrier, inc=1, device_id=(owner_of(i), t), device_id_type=MESH)
        return carry

    lax.fori_loop(1, owners, greet, 0)

    def greet_t(j, carry):
        pl.semaphore_signal(barrier, inc=1, device_id=(me, (t + j) % ts), device_id_type=MESH)
        return carry

    lax.fori_loop(1, ts, greet_t, 0)

    for one in loads[1:6]:
        one.wait()

    adapters = store_ref.shape[1]
    hits = (iota((adapters, count), 0) == dec_index_ref[...]).astype(F32).astype(BF16)
    table = jnp.broadcast_to(store_ref[...], (8, adapters)).astype(F32).astype(BF16)
    slot = nn_dot(table, hits)[0:1].astype(I32)
    owner, local = slot // 2, slot % 2
    dz = (owner // xs - z + zs) % zs
    dx = (owner % xs - x + xs) % xs
    half = (dz >= zs // 2).astype(I32)
    k = jnp.where(dz < zs // 2, dz, jnp.where(dz == zs // 2, 0, zs - dz))
    block = k * wide + half * xs + dx
    square = (count, count)
    block_rows = jnp.broadcast_to(block, square)
    block_cols = jnp.transpose(block_rows.astype(F32)).astype(I32)
    same = jnp.logical_and(block_rows == block_cols, iota(square, 0) < iota(square, 1))
    before = jnp.sum(same.astype(F32), axis=0, keepdims=True).astype(I32)
    place = block * BLOCK + before
    code = jnp.broadcast_to(place * 2 + local, square)
    code_cols = jnp.transpose(code.astype(F32)).astype(I32)
    place_cols = code_cols // 2
    named = (code_cols % 2 + 1).astype(F32)
    lanes = iota((count, 128), 1)
    slot_cols = jnp.broadcast_to(place_cols[:, 0:1] % BLOCK, (count, 128))
    spread = jnp.where(
        lanes % DEPTH == slot_cols, jnp.broadcast_to(named[:, 0:1], (count, 128)), 0.0
    )
    in_block = (iota((owners, count), 0) == block).astype(F32).astype(BF16)
    meta2[...] = nn_dot(in_block, spread.astype(BF16))

    def lift(i, carry):
        meta_send[i] = meta2[pl.ds(i, 1), :]
        return carry

    lax.fori_loop(0, owners, lift, 0)
    meta_got[0] = meta2[0:1, :]

    loads[0].wait()
    pl.semaphore_wait(barrier, owners - 1 + ts - 1)

    def row_copy(i):
        at = pl.ds(pl.multiple_of(i * BLOCK, BLOCK), BLOCK)
        return pltpu.make_async_remote_copy(
            src_ref=send.at[at],
            dst_ref=got.at[at],
            send_sem=send_sem,
            recv_sem=got_sems.at[i // wide],
            device_id=(owner_of(i), t),
            device_id_type=MESH,
        )

    def meta_copy(i):
        return pltpu.make_async_remote_copy(
            src_ref=meta_send.at[i],
            dst_ref=meta_got.at[i],
            send_sem=meta_send_sem,
            recv_sem=meta_got_sems.at[i // wide],
            device_id=(owner_of(i), t),
            device_id_type=MESH,
        )

    def start_rows(i, carry):
        meta_copy(i).start()
        row_copy(i).start()
        return carry

    def dispatch(g):
        base = pl.multiple_of(g * gr, gr)
        rel = iota((gr, count), 0) + base
        sum_rows = jnp.zeros((gr, wc), F32)
        for c in range(CHUNKS):
            chosen = (rel == place + c * DEPTH).astype(F32).astype(BF16)
            sum_rows += nn_dot(chosen, dec[:, c * wc : (c + 1) * wc])
        send[pl.ds(base, gr), :] = sum_rows.astype(BF16)

    dispatch(0)
    lax.fori_loop(1, wide, start_rows, 0)
    got[0:BLOCK, :] = send[0:BLOCK, :]

    def dispatch_more(g, carry):
        dispatch(g)
        lax.fori_loop(g * wide, (g + 1) * wide, start_rows, 0)
        return carry

    lax.fori_loop(1, groups, dispatch_more, 0)

    step = dz
    flow = block // xs
    earlier = jnp.logical_or(
        block_cols < block_rows,
        jnp.logical_and(block_cols == block_rows, iota(square, 0) < iota(square, 1)),
    )
    mates = jnp.logical_and(block_cols // xs == block_rows // xs, earlier)
    queue = jnp.sum(mates.astype(F32), axis=0, keepdims=True).astype(I32)
    more = jnp.transpose(jnp.broadcast_to(step * 8 + before, square).astype(F32)).astype(I32)
    step_col, slot_col = more[:, 0:1] // 8, more[:, 0:1] % 8
    ring = iota((count, 128), 1) % zs
    load_of = jnp.sum((ring == step_col).astype(F32), axis=0, keepdims=True)

    def from_next(v):
        return pltpu.roll(v, 127, 1)

    def from_last(v):
        return pltpu.roll(v, 1, 1)

    load_of = jnp.broadcast_to(load_of, (8, 128))
    above, below = from_next(load_of), from_last(load_of)
    rest = jnp.maximum(load_of - KEPT, 0.0)
    moved = []
    for way, top in MOVES:
        can = ((above if way > 0 else below) <= top).astype(F32)
        if len(moved) == 2:
            can = can * (1.0 - from_last(from_last(moved[0])))
        if len(moved) == 3:
            can = can * (1.0 - from_next(from_next(moved[1])))
        now = jnp.where(rest > 0, can, 0.0)
        rest = rest - now
        moved.append(now)
    stuck = jnp.max(rest, axis=1, keepdims=True)
    row8 = iota((8, 128), 0)
    leave = jnp.zeros((8, 128), F32)
    enter = jnp.zeros((8, 128), F32)
    for m, (way, _) in enumerate(MOVES):
        leave = jnp.where(row8 == m, moved[m], leave)
        enter = jnp.where(row8 == m, from_last(moved[m]) if way > 0 else from_next(moved[m]), enter)
    at_step = (iota((128, count), 0) == step).astype(F32).astype(BF16)
    mine = nn_dot(leave.astype(BF16), at_step)
    code = jnp.where(queue < KEPT, queue + 1, 0)
    home_step, home_slot = step, queue
    seen = jnp.zeros((1, count), F32)
    over = (queue - KEPT).astype(F32)
    for m, (way, top) in enumerate(MOVES):
        used = mine[m : m + 1]
        hit = jnp.where(over == seen, used, 0.0) > 0.5
        code = jnp.where(hit, KEPT + 1 + m, code)
        home_step = jnp.where(hit, (step + zs + way) % zs, home_step)
        home_slot = jnp.where(hit, top, home_slot)
        seen = seen + used
    home_far = (home_step >= zs // 2).astype(I32)
    home_k = jnp.where(
        home_step < zs // 2, home_step, jnp.where(home_step == zs // 2, 0, zs - home_step)
    )
    home = jnp.where(code > 0, (2 * home_k + home_far) * 16 + home_slot, 4095)
    home_cols = jnp.transpose(jnp.broadcast_to(home, square).astype(F32)).astype(I32)[:, 0:1]
    code_col = jnp.transpose(jnp.broadcast_to(code, square).astype(F32))[:, 0:1]
    block_col = block_cols[:, 0:1]
    lane_x = lanes // BLOCK
    lane_r = lanes % DEPTH
    fits = jnp.logical_and(lane_x == block_col % xs, lane_r == slot_col)
    codes = jnp.where(fits, jnp.broadcast_to(code_col, (count, 128)), 0.0).astype(BF16)
    in_flow = (iota((zs, count), 0) == flow).astype(F32).astype(BF16)
    signs = jnp.concatenate(
        [
            jnp.zeros((64, 128), F32),
            leave,
            enter,
            jnp.broadcast_to(stuck, (8, 128)),
            jnp.zeros((40, 128), F32),
        ],
        axis=0,
    )
    signs = jnp.transpose(signs).astype(BF16)
    fi = iota((zs, 128), 0)
    f_near = fi // 2
    f_step = jnp.where(
        fi % 2 == 0, f_near, jnp.where(f_near == 0, zs // 2, zs - f_near)
    )
    pick = (f_step == iota((zs, 128), 1)).astype(F32).astype(BF16)
    rmeta2[...] = nn_dot(in_flow, codes) + nn_dot(pick, signs)

    def lift_plan(f, carry):
        rmeta_send[f] = rmeta2[pl.ds(f, 1), :]
        return carry

    lax.fori_loop(0, zs, lift_plan, 0)
    rmeta_got[0] = rmeta2[0:1, :]

    def start_plan(f, carry):
        pltpu.make_async_remote_copy(
            src_ref=rmeta_send.at[f],
            dst_ref=rmeta_got.at[f],
            send_sem=rmeta_send_sem,
            recv_sem=rmeta_got_sem,
            device_id=(z_peer(flow_step(f)), t),
            device_id_type=MESH,
        ).start()
        return carry

    lax.fori_loop(1, zs, start_plan, 0)

    rank = down.shape[0] // 2
    learn = rows.shape[0]
    own_slot = store_s_ref[blk_s_ref[0]] % 2
    aj = iota((learn, 2 * rank), 1)
    own = (aj // rank == own_slot).astype(F32)
    loads[6].wait()
    loads[7].wait()
    forward = nt_dot(rows[...], down[...]) * own
    loads[8].wait()
    loads[9].wait()
    backward = nt_dot(grad[...], up[...]) * own
    forward = forward + pltpu.roll(forward, rank, 1)
    backward = backward + pltpu.roll(backward, rank, 1)
    lpart[...] = jnp.where(aj < rank, forward, backward)

    def lpart_copy(j):
        return pltpu.make_async_remote_copy(
            src_ref=lpart,
            dst_ref=lpart_got.at[j - 1],
            send_sem=lpart_send_sem,
            recv_sem=lpart_got_sem,
            device_id=(me, (t + j) % ts),
            device_id_type=MESH,
        )

    def start_lpart(j, carry):
        lpart_copy(j).start()
        return carry

    lax.fori_loop(1, ts, start_lpart, 0)

    def wait_group(g, ref, size, sems):
        @pl.when(g == 0)
        def _():
            view = ref.at[pl.ds(size, (wide - 1) * size)]
            pltpu.make_async_copy(view, view, sems.at[g]).wait()

        @pl.when(g > 0)
        def _():
            view = ref.at[pl.ds(pl.multiple_of(g * wide * size, wide * size), wide * size)]
            pltpu.make_async_copy(view, view, sems.at[g]).wait()

    chunk_of = (iota((gr, 2 * rank), 0) % BLOCK) // DEPTH
    lane = iota((gr, 2 * rank), 1)

    def chosen_mask(g):
        ids = meta_got[pl.ds(g * wide, wide)]
        ids = jnp.broadcast_to(ids, (wide, BLOCK, 128)).reshape(gr, 128)
        mine = iota((gr, 128), 1) == iota((gr, 128), 0) % DEPTH
        which = jnp.sum(jnp.where(mine, ids, 0.0), axis=1, keepdims=True)
        return (which == (lane // rank + 1).astype(F32)).astype(F32)

    pairs = wide // 2
    top3 = iota((wide, 8, 2 * rank), 1) < DEPTH
    left3 = iota((wide, 8, 2 * rank), 2) < rank

    def part_copy(g, j):
        return pltpu.make_async_remote_copy(
            src_ref=part.at[g],
            dst_ref=part_got.at[g, j - 1],
            send_sem=part_send_sem,
            recv_sem=part_got_sems.at[g],
            device_id=(me, (t + j) % ts),
            device_id_type=MESH,
        )

    def ranks(g):
        wait_group(g, got, BLOCK, got_sems)
        wait_group(g, meta_got, 1, meta_got_sems)
        at = pl.ds(pl.multiple_of(g * gr, gr), gr)
        block_rows = got[at, :]
        both = jnp.zeros((gr, 2 * rank), F32)
        for c in range(CHUNKS):
            one = nt_dot(block_rows, down[:, c * wc : (c + 1) * wc])
            both = both + jnp.where(chunk_of == c, one, 0.0)
        both = both * chosen_mask(g)
        both = both.reshape(wide, 2, 8, 2 * rank)
        both = both[:, 0] + both[:, 1]
        both = both + pltpu.roll(both, DEPTH, 1)
        both = both + pltpu.roll(both, rank, 2)
        both = both.reshape(2, pairs, 8, 2 * rank)
        two = jnp.where(top3[:pairs], both[0], both[1])
        two = two.reshape(2, pairs // 2, 8, 2 * rank)
        part[g] = jnp.where(left3[: pairs // 2], two[0], two[1])

        def start(j, carry):
            part_copy(g, j).start()
            return carry

        lax.fori_loop(1, ts, start, 0)

    def start_cross(g):
        for half in range(2):
            for dx in range(xs):
                row = (g * wide + half * xs + dx) * BLOCK
                at = pl.ds(pl.multiple_of(row, BLOCK), BLOCK)
                if dx == 0:
                    pltpu.make_async_copy(dsend.at[at], xgot.at[at], xgot_sems.at[g]).start()
                else:
                    pltpu.make_async_remote_copy(
                        src_ref=dsend.at[at],
                        dst_ref=xgot.at[at],
                        send_sem=xsend_sem,
                        recv_sem=xgot_sems.at[g],
                        device_id=(x_peer(xs - dx), t),
                        device_id_type=MESH,
                    ).start()

    def deltas(g):
        view = part_got.at[g]
        pltpu.make_async_copy(view, view, part_got_sems.at[g]).wait()
        v = part[g]
        for j in range(ts - 1):
            v = v + part_got[g, j]
        v = (v * shrink).astype(BF16).astype(F32)
        turned = pltpu.roll(v, rank, 2)
        keep = left3[: pairs // 2]
        two = jnp.concatenate([jnp.where(keep, v, turned), jnp.where(keep, turned, v)], axis=0)
        turned = pltpu.roll(two, DEPTH, 1)
        keep = top3[:pairs]
        both = jnp.concatenate([jnp.where(keep, two, turned), jnp.where(keep, turned, two)], axis=0)
        both = jnp.broadcast_to(both[:, None], (wide, 2, 8, 2 * rank)).reshape(gr, 2 * rank)
        both = both * chosen_mask(g)
        base = pl.multiple_of(g * gr, gr)
        sum_rows = jnp.zeros((gr, hc), F32)
        for c in range(CHUNKS):
            left = jnp.where(chunk_of == c, both, 0.0).astype(BF16)
            sum_rows += nn_dot(left, up[:, c * hc : (c + 1) * hc])
        dsend[pl.ds(base, gr), :] = (sum_rows * expand).astype(BF16)

        start_cross(g)

    def read_plans():
        view = rmeta_got.at[pl.ds(1, zs - 1)]
        pltpu.make_async_copy(view, view, rmeta_got_sem).wait()
        plan = rmeta_got[...].reshape(zs, 128)
        lane16 = iota((zs, 128), 1)
        source = (z + zs - f_step) % zs
        other_f = iota((zs, zs), 1)
        other_near = other_f // 2
        other_step = jnp.where(
            other_f % 2 == 0, other_near, jnp.where(other_near == 0, zs // 2, zs - other_near)
        )
        other = (z + zs - other_step) % zs
        first = (other < source[:, 0:1]).astype(F32).astype(BF16)
        ahead = nn_dot(first, plan.astype(BF16))

        def column(v, n):
            return jnp.sum(jnp.where(lane16 == n, v, 0.0), axis=1, keepdims=True)

        def places(base, order):
            here = [column(plan, base + m) for m in order]
            at = column(ahead, base + order[0])
            for m in order[1:]:
                at = at + column(ahead, base + m)
            out = []
            for one in here:
                out.append(jnp.where(one > 0.5, at, -1.0))
                at = at + one
            return out, at

        ups = [m for m, (way, _) in enumerate(MOVES) if way > 0]
        downs = [m for m, (way, _) in enumerate(MOVES) if way < 0]
        t_slot[...] = jnp.where(plan < KEPT + 0.5, plan - 1.0, -1.0)
        worst = column(plan, 80)
        for table, order in ((t_plus, ups), (t_minus, downs)):
            spots, end = places(64, order)
            worst = jnp.maximum(worst, jnp.where(end > SPARE + 0.5, 1.0, 0.0))
            value = jnp.full((zs, 128), -1.0, F32)
            for m, spot in zip(order, spots):
                value = jnp.where(plan == KEPT + 1.0 + m, spot, value)
            table[...] = value
        value = jnp.full((zs, 128), -1.0, F32)
        spot_lane = (lane16 % SPARE).astype(F32)
        side_lane = lane16 // (SPARE * CHUNKS)
        for side, order in ((0, ups), (1, downs)):
            spots, _ = places(72, order)
            for m, spot in zip(order, spots):
                hit = jnp.logical_and(side_lane == side, spot_lane == spot)
                value = jnp.where(hit, MOVES[m][1] - 8.0, value)
        t_in[...] = value
        worst = jnp.max(worst, axis=0, keepdims=True)
        flag_send[...] = jnp.broadcast_to(worst, (1, 128))
        flag_got[0] = flag_send[...]

        def start(f, carry):
            pltpu.make_async_remote_copy(
                src_ref=flag_send,
                dst_ref=flag_got.at[f],
                send_sem=flag_sems.at[0],
                recv_sem=flag_sems.at[1],
                device_id=(z_peer(flow_step(f)), t),
                device_id_type=MESH,
            ).start()
            return carry

        lax.fori_loop(1, zs, start, 0)
        spill[...] = jnp.zeros_like(spill)

    def pick_rows(table, f, per, cells):
        shape = (per * CHUNKS, cells)
        wanted = (iota(shape, 0) % per).astype(F32)
        here = jnp.broadcast_to(table[pl.ds(f, 1), :][:, :cells], shape)
        return here, wanted, iota(shape, 0) // per

    cells = xs * BLOCK
    kept_a, kept_b = 8 * CHUNKS, DEPTH * CHUNKS

    def a_copy(f):
        at = pl.ds(pl.multiple_of(f * kept_a, kept_a), kept_a)
        return pltpu.make_async_remote_copy(
            src_ref=asend.at[at],
            dst_ref=agot.at[at],
            send_sem=asend_sem,
            recv_sem=agot_sems.at[f // 2],
            device_id=(z_peer(zs - flow_step(f)), t),
            device_id_type=MESH,
        )

    def start_a(f, carry):
        a_copy(f).start()
        return carry

    held_back = min(3, groups - 1)

    def relay(g):
        view = xgot.at[pl.ds(pl.multiple_of(g * gr, gr), gr)]
        pltpu.make_async_copy(view, view, xgot_sems.at[g]).wait()

        def one_flow(f, carry):
            chunk = (iota((1, cells), 1) % BLOCK) // DEPTH
            picks = []
            for table, per, base in (
                (t_slot, 8, 0.0),
                (t_slot, DEPTH, 8.0),
                (t_plus, SPARE, 0.0),
                (t_minus, SPARE, 0.0),
            ):
                here, wanted, c = pick_rows(table, f, per, cells)
                hit = jnp.logical_and(here == wanted + base, chunk == c)
                picks.append(hit.astype(F32))
            picks = jnp.concatenate(picks, axis=0).astype(BF16)
            blocks = xgot[pl.ds(pl.multiple_of(f * cells, cells), cells), :]
            packed = nn_dot(picks, blocks)
            asend[pl.ds(pl.multiple_of(f * kept_a, kept_a), kept_a), :] = packed[:kept_a].astype(BF16)
            bsend[pl.ds(pl.multiple_of(f * kept_b, kept_b), kept_b), :] = packed[
                kept_a : kept_a + kept_b
            ].astype(BF16)
            spill[...] += packed[kept_a + kept_b :]
            return carry

        lax.fori_loop(2 * g, 2 * g + 2, one_flow, 0)

        @pl.when(g == 0)
        def _():
            agot[0:kept_a, :] = asend[0:kept_a, :]
            lax.fori_loop(1, 2, start_a, 0)

        @pl.when(jnp.logical_and(g > 0, g < groups - held_back))
        def _():
            lax.fori_loop(2 * g, 2 * g + 2, start_a, 0)

    def stage(s, carry):
        @pl.when(s < groups)
        def _():
            ranks(s)

        @pl.when(s == 1)
        def _():
            read_plans()

        @pl.when(jnp.logical_and(s >= 1, s < groups + 1))
        def _():
            deltas(s - 1)

        @pl.when(s >= 2)
        def _():
            relay(s - 2)

        return carry

    lax.fori_loop(0, groups + 2, stage, 0)

    spare = SPARE * CHUNKS
    fsend[...] = spill[...].astype(BF16)
    for side, way in ((0, 1), (1, zs - 1)):
        at = pl.ds(side * spare, spare)
        pltpu.make_async_remote_copy(
            src_ref=fsend.at[at],
            dst_ref=fgot.at[at],
            send_sem=fsend_sem,
            recv_sem=fgot_sem,
            device_id=(z_peer(way), t),
            device_id_type=MESH,
        ).start()
    lax.fori_loop(2 * (groups - held_back), 2 * groups, start_a, 0)

    pltpu.make_async_copy(lpart_got, lpart_got, lpart_got_sem).wait()
    v = lpart[...]
    for j in range(ts - 1):
        v = v + lpart_got[j]
    live = (iota((learn, 2 * rank), 0) < live_s_ref[0]).astype(F32)
    scale = jnp.where(aj < rank, shrink, expand)
    v = (v * scale * live).astype(BF16).astype(F32)
    turned = pltpu.roll(v, rank, 1)
    act = (jnp.where(aj < rank, v, turned) * own).astype(BF16)
    back = (jnp.where(aj < rank, turned, v) * own).astype(BF16)
    for c in range(CHUNKS):
        at = slice(c * wc, (c + 1) * wc)
        g_a = tn_dot(back, rows[:, at]) * shrink
        down_out[:, at] = (down[:, at].astype(F32) - DOWN_RATE * g_a).astype(BF16)
    for c in range(CHUNKS):
        at = slice(c * hc, (c + 1) * hc)
        g_b = tn_dot(act, grad[:, at]) * expand
        up_out[:, at] = (up[:, at].astype(F32) - UP_RATE * g_b).astype(BF16)

    pltpu.make_async_copy(fgot, fgot, fgot_sem).wait()

    def b_copy(f):
        at = pl.ds(pl.multiple_of(f * kept_b, kept_b), kept_b)
        return pltpu.make_async_remote_copy(
            src_ref=bsend.at[at],
            dst_ref=bgot.at[at],
            send_sem=bsend_sem,
            recv_sem=bgot_sems.at[f // 4],
            device_id=(z_peer(zs - flow_step(f)), t),
            device_id_type=MESH,
        )

    def finish_b(f, carry):
        here, wanted, c = pick_rows(t_in, f, DEPTH, 2 * spare)
        chunk = (iota((1, 2 * spare), 1) % spare) // SPARE
        hit = jnp.logical_and(here == wanted, chunk == c)
        at = pl.ds(pl.multiple_of(f * kept_b, kept_b), kept_b)
        extra = nn_dot(hit.astype(F32).astype(BF16), fgot[...])
        bsend[at, :] = (bsend[at, :].astype(F32) + extra).astype(BF16)

        @pl.when(f > 0)
        def _():
            b_copy(f).start()

        return carry

    lax.fori_loop(0, zs, finish_b, 0)
    bgot[0:kept_b, :] = bsend[0:kept_b, :]

    pltpu.make_async_copy(
        flag_got.at[pl.ds(1, zs - 1)], flag_got.at[pl.ds(1, zs - 1)], flag_sems.at[1]
    ).wait()
    worst = flag_got[0]
    for f in range(1, zs):
        worst = jnp.maximum(worst, flag_got[f])
    flagx_send[...] = worst
    for dx in range(1, xs):
        pltpu.make_async_remote_copy(
            src_ref=flagx_send,
            dst_ref=flagx_got.at[dx - 1],
            send_sem=flag_sems.at[2],
            recv_sem=flag_sems.at[3],
            device_id=(x_peer(dx), t),
            device_id_type=MESH,
        ).start()

    total[...] = jnp.zeros_like(total)
    pair = 2 * kept_a
    home_flow = jnp.broadcast_to(home_cols // 16, (count, pair))
    home_slot = jnp.broadcast_to(home_cols % 16, (count, pair))
    in_a = home_slot < 8
    place_a = jnp.where(in_a, home_flow * kept_a + home_slot, -4096)
    place_b = jnp.where(in_a, -4096, home_flow * kept_b + home_slot - 8)

    def add_up(ref, g, place, chunk_rows):
        base = pl.multiple_of(g * pair, pair)
        rel = iota((count, pair), 1) + base
        arrived = ref[pl.ds(base, pair), :]
        for c in range(CHUNKS):
            chosen = (rel == place + c * chunk_rows).astype(F32).astype(BF16)
            total[:, c * hc : (c + 1) * hc] += nn_dot(chosen, arrived)

    def wait_pair(ref, g, own, sems):
        @pl.when(g == 0)
        def _():
            view = ref.at[pl.ds(own, pair - own)]
            pltpu.make_async_copy(view, view, sems.at[g]).wait()

        @pl.when(g > 0)
        def _():
            view = ref.at[pl.ds(pl.multiple_of(g * pair, pair), pair)]
            pltpu.make_async_copy(view, view, sems.at[g]).wait()

    def combine_a(g, carry):
        wait_pair(agot, g, kept_a, agot_sems)
        add_up(agot, g, place_a, 8)
        return carry

    lax.fori_loop(0, groups, combine_a, 0)

    def combine_b(g, carry):
        wait_pair(bgot, g, kept_b, bgot_sems)
        add_up(bgot, g, place_b, DEPTH)
        return carry

    lax.fori_loop(0, zs // 4, combine_b, 0)
    delta_out[...] = total[...].astype(BF16)
    pltpu.make_async_copy(flagx_got, flagx_got, flag_sems.at[3]).wait()
    worst = flagx_send[...]
    for dx in range(1, xs):
        worst = jnp.maximum(worst, flagx_got[dx - 1])
    flag_out[...] = jnp.broadcast_to(worst, (8, 128))

    def drain(view, sem):
        pltpu.make_async_copy(view, view, sem).wait()

    drain(send.at[pl.ds(BLOCK, (owners - 1) * BLOCK)], send_sem)
    drain(meta_send.at[pl.ds(1, owners - 1)], meta_send_sem)
    drain(dsend.at[pl.ds(0, zs * (xs - 1) * BLOCK)], xsend_sem)
    drain(rmeta_send.at[pl.ds(1, zs - 1)], rmeta_send_sem)
    drain(asend.at[pl.ds(kept_a, (zs - 1) * kept_a)], asend_sem)
    drain(bsend.at[pl.ds(kept_b, (zs - 1) * kept_b)], bsend_sem)
    drain(fsend, fsend_sem)
    drain(flag_got.at[pl.ds(1, zs - 1)], flag_sems.at[0])
    drain(flagx_got, flag_sems.at[2])
    drain(lpart_got, lpart_send_sem)
    drain(part_got, part_send_sem)


def lookup(table, wanted):
    hits = wanted[:, None] == jnp.arange(table.shape[0], dtype=jnp.int32)[None, :]
    return jnp.sum(jnp.where(hits, table[None, :], 0), axis=1)


def padded_exchange(
    decode_input_rows,
    decode_adapter_index,
    adapter_storage_index,
    adapter_down_weight,
    adapter_up_weight,
):
    owners = lax.axis_size("dp")
    split_points = lax.axis_size("tensor")
    holder_mask, rank_extent, width_portion = adapter_down_weight.shape
    hidden_portion = adapter_up_weight.shape[2]
    shrink = (width_portion * split_points) ** (-0.5)
    expand = rank_extent ** (-0.5)
    row_count = decode_input_rows.shape[0]
    slot_depth = 2 * row_count // owners
    total_slots = owners * slot_depth
    slot_row = lookup(adapter_storage_index, decode_adapter_index)
    target = slot_row // holder_mask
    local_slot = slot_row % holder_mask
    target_hot = (target[:, None] == jnp.arange(owners, dtype=jnp.int32)[None, :]).astype(jnp.int32)
    before = jnp.cumsum(target_hot, axis=0) - target_hot
    position = target * slot_depth + jnp.sum(before * target_hot, axis=1)
    matches = jnp.arange(total_slots, dtype=jnp.int32)[:, None] == position[None, :]
    dispatch = matches.astype(jnp.bfloat16)
    send_rows = jnp.dot(dispatch, decode_input_rows, preferred_element_type=jnp.float32).astype(
        jnp.bfloat16
    )
    filled = jnp.any(matches, axis=1)
    send_local = jnp.where(filled, jnp.sum(jnp.where(matches, local_slot[None, :], 0), axis=1), -1)
    send_rows = send_rows.reshape(owners, slot_depth, width_portion)
    send_local = send_local.astype(jnp.bfloat16).reshape(owners, slot_depth)
    flattened_second = adapter_up_weight.reshape(holder_mask * rank_extent, hidden_portion)
    got_rows, got_local = (
        lax.all_to_all(send_rows, "dp", split_axis=0, concat_axis=0, tiled=True),
        lax.all_to_all(send_local, "dp", split_axis=0, concat_axis=0, tiled=True),
    )
    sources, items = got_local.shape
    flattened_rows = got_rows.reshape(sources * items, width_portion)
    which_slot = got_local.reshape(-1).astype(jnp.float32)
    chosen = (which_slot[:, None] == jnp.arange(holder_mask, dtype=jnp.float32)[None, :]).astype(
        jnp.float32
    )
    partial_output = jnp.einsum(
        "lm,kjm->lkj", flattened_rows, adapter_down_weight, preferred_element_type=jnp.float32
    )
    to_sum = partial_output.reshape(sources * items, holder_mask * rank_extent)
    summed = lax.psum(to_sum, "tensor")
    spread = summed.reshape(sources * items, holder_mask, rank_extent) * chosen[:, :, None]
    hidden = (
        (spread * shrink).reshape(sources * items, holder_mask * rank_extent).astype(jnp.bfloat16)
    )
    delta_rows = jnp.dot(hidden, flattened_second, preferred_element_type=jnp.float32) * expand
    answer = delta_rows.astype(jnp.bfloat16).reshape(sources, items, hidden_portion)
    returned = lax.all_to_all(answer, "dp", split_axis=0, concat_axis=0, tiled=True)
    merged = returned.reshape(total_slots, hidden_portion)
    dec_delta = jnp.einsum(
        "mr,mf->rf", dispatch, merged, preferred_element_type=jnp.float32
    ).astype(jnp.bfloat16)
    return dec_delta


def local(
    decode_input_rows,
    decode_adapter_index,
    adapter_storage_index,
    learner_input_rows,
    learner_gradient,
    block_adapter_index,
    block_live_count,
    adapter_down_weight,
    adapter_up_weight,
):
    owners = lax.axis_size("dp")
    ts = lax.axis_size("tensor")
    xs = 4
    zs = owners // xs
    held, rank, width = adapter_down_weight.shape
    hidden = adapter_up_weight.shape[2]
    count = decode_input_rows.shape[0]
    learn = learner_input_rows.shape[0]
    shrink = (width * ts) ** (-0.5)
    expand = rank ** (-0.5)
    groups = zs // 2
    wide = 2 * xs
    vmem = pl.BlockSpec(memory_space=pltpu.VMEM)
    hbm = pl.BlockSpec(memory_space=pltpu.HBM)
    dma = pltpu.SemaphoreType.DMA
    packed = (wide // 4, 8, 2 * rank)
    rows_a, rows_b, spare = 8 * CHUNKS, DEPTH * CHUNKS, SPARE * CHUNKS
    chunk = hidden // CHUNKS
    delta, down, up, flag = pl.pallas_call(
        functools.partial(kernel, (zs, xs, ts, shrink, expand)),
        out_shape=(
            jax.ShapeDtypeStruct((count, hidden), BF16),
            jax.ShapeDtypeStruct((held * rank, width), BF16),
            jax.ShapeDtypeStruct((held * rank, hidden), BF16),
            jax.ShapeDtypeStruct((8, 128), F32),
        ),
        in_specs=[hbm] * 10,
        out_specs=(vmem, vmem, vmem, vmem),
        scratch_shapes=[
            pltpu.VMEM((1, count), I32),
            pltpu.VMEM((1, adapter_storage_index.shape[0]), I32),
            pltpu.SMEM((adapter_storage_index.shape[0],), I32),
            pltpu.SMEM((1,), I32),
            pltpu.SMEM((1,), I32),
            pltpu.VMEM((count, width), BF16),
            pltpu.VMEM((learn, width), BF16),
            pltpu.VMEM((learn, hidden), BF16),
            pltpu.VMEM((held * rank, width), BF16),
            pltpu.VMEM((held * rank, hidden), BF16),
            pltpu.VMEM((owners * BLOCK, width // CHUNKS), BF16),
            pltpu.VMEM((owners * BLOCK, width // CHUNKS), BF16),
            pltpu.VMEM((owners, 128), F32),
            pltpu.VMEM((owners, 1, 128), F32),
            pltpu.VMEM((owners, 1, 128), F32),
            pltpu.VMEM((groups,) + packed, F32),
            pltpu.VMEM((groups, ts - 1) + packed, F32),
            pltpu.VMEM((learn, 2 * rank), F32),
            pltpu.VMEM((ts - 1, learn, 2 * rank), F32),
            pltpu.VMEM((owners * BLOCK, chunk), BF16),
            pltpu.VMEM((owners * BLOCK, chunk), BF16),
            pltpu.VMEM((zs, 128), F32),
            pltpu.VMEM((zs, 1, 128), F32),
            pltpu.VMEM((zs, 1, 128), F32),
            pltpu.VMEM((zs, 128), F32),
            pltpu.VMEM((zs, 128), F32),
            pltpu.VMEM((zs, 128), F32),
            pltpu.VMEM((zs, 128), F32),
            pltpu.VMEM((zs * rows_a, chunk), BF16),
            pltpu.VMEM((zs * rows_a, chunk), BF16),
            pltpu.VMEM((zs * rows_b, chunk), BF16),
            pltpu.VMEM((zs * rows_b, chunk), BF16),
            pltpu.VMEM((2 * spare, chunk), F32),
            pltpu.VMEM((2 * spare, chunk), BF16),
            pltpu.VMEM((2 * spare, chunk), BF16),
            pltpu.VMEM((1, 128), F32),
            pltpu.VMEM((zs, 1, 128), F32),
            pltpu.VMEM((1, 128), F32),
            pltpu.VMEM((xs - 1, 1, 128), F32),
            pltpu.VMEM((count, hidden), F32),
            dma((10,)),
            dma,
            dma((groups,)),
            dma,
            dma((groups,)),
            dma,
            dma((groups,)),
            dma,
            dma,
            dma,
            dma((groups,)),
            dma,
            dma,
            dma,
            dma((groups,)),
            dma,
            dma((zs // 4,)),
            dma,
            dma,
            dma((4,)),
        ],
        compiler_params=pltpu.CompilerParams(
            collective_id=0, has_side_effects=True, vmem_limit_bytes=58 * 1024 * 1024
        ),
    )(
        decode_adapter_index.reshape(1, count),
        adapter_storage_index.reshape(1, -1),
        adapter_storage_index,
        block_adapter_index,
        block_live_count,
        decode_input_rows,
        learner_input_rows,
        learner_gradient,
        adapter_down_weight.reshape(held * rank, width),
        adapter_up_weight.reshape(held * rank, hidden),
    )
    def padded():
        return padded_exchange(
            decode_input_rows,
            decode_adapter_index,
            adapter_storage_index,
            adapter_down_weight,
            adapter_up_weight,
        )

    delta = lax.cond(flag[0, 0] > 0.5, padded, lambda: delta)
    return delta, down.reshape(held, rank, width), up.reshape(held, rank, hidden)


def solution(mesh):
    in_specs = (
        P("dp", "tensor"),
        P("dp"),
        P(),
        P("dp", "tensor"),
        P("dp", "tensor"),
        P("dp"),
        P("dp"),
        P("dp", None, "tensor"),
        P("dp", None, "tensor"),
    )
    out_specs = (P("dp", "tensor"), P("dp", None, "tensor"), P("dp", None, "tensor"))
    return jax.shard_map(local, mesh=mesh, in_specs=in_specs, out_specs=out_specs, check_vma=False)
```

```python
import functools

import jax
import jax.numpy as jnp
from jax import lax
from jax.experimental import pallas as pl
from jax.experimental.pallas import tpu as pltpu
from jax.sharding import PartitionSpec as P

DOWN_RATE = 4.0
UP_RATE = 0.25
DEPTH = 4
CHUNKS = 4
BLOCK = DEPTH * CHUNKS
KEPT = 12
SPARE = 8
MOVES = ((1, 11), (-1, 10), (-1, 11), (1, 10), (1, 9), (-1, 8))
VMEM_LIMIT = 58 * 1024 * 1024
MESH = pl.DeviceIdType.MESH
F32, BF16, I32 = jnp.float32, jnp.bfloat16, jnp.int32


def nt_dot(a, b):
    return lax.dot_general(a, b, (((1,), (1,)), ((), ())), preferred_element_type=F32)


def tn_dot(a, b):
    return lax.dot_general(a, b, (((0,), (0,)), ((), ())), preferred_element_type=F32)


def nn_dot(a, b):
    return jnp.dot(a, b, preferred_element_type=F32)


def iota(shape, axis):
    return lax.broadcasted_iota(I32, shape, axis)


def kernel(
    geometry,
    dec_index_hbm,
    store_hbm,
    store_flat_hbm,
    blk_hbm,
    live_hbm,
    dec_hbm,
    rows_hbm,
    grad_hbm,
    down_hbm,
    up_hbm,
    delta_out,
    down_out,
    up_out,
    flag_out,
    dec_index_ref,
    store_ref,
    store_s_ref,
    blk_s_ref,
    live_s_ref,
    dec,
    rows,
    grad,
    down,
    up,
    send,
    got,
    meta2,
    meta_send,
    meta_got,
    part,
    part_got,
    lpart,
    lpart_got,
    dsend,
    xgot,
    rmeta2,
    rmeta_send,
    rmeta_got,
    t_slot,
    t_plus,
    t_minus,
    t_in,
    asend,
    agot,
    bsend,
    bgot,
    spill,
    fsend,
    fgot,
    flag_send,
    flag_got,
    flagx_send,
    flagx_got,
    total,
    load_sems,
    send_sem,
    got_sems,
    meta_send_sem,
    meta_got_sems,
    part_send_sem,
    part_got_sems,
    lpart_send_sem,
    lpart_got_sem,
    xsend_sem,
    xgot_sems,
    rmeta_send_sem,
    rmeta_got_sem,
    asend_sem,
    agot_sems,
    bsend_sem,
    bgot_sems,
    fsend_sem,
    fgot_sem,
    flag_sems,
):
    zs, xs, ts, shrink, expand = geometry
    owners = zs * xs
    wide = 2 * xs
    groups = zs // 2
    gr = wide * BLOCK
    me = lax.axis_index("dp")
    t = lax.axis_index("tensor")
    z, x = lax.div(me, xs), lax.rem(me, xs)
    count = dec.shape[0]
    wc = dec.shape[1] // CHUNKS
    hc = grad.shape[1] // CHUNKS

    x_at = [lax.rem(x + dx, xs) for dx in range(xs)]
    t_at = [lax.rem(t + j, ts) for j in range(ts)]

    def flow_step(f):
        near = lax.rem(zs // 2 - lax.div(f, 2), zs // 2)
        return near + lax.rem(f, 2) * (zs - 2 * near - (zs // 2) * lax.div(zs - near, zs))

    def x_peer(dx):
        return z * xs + x_at[dx]

    def z_peer(dz):
        return lax.rem(z + dz, zs) * xs + x

    def z_row(f):
        return lax.rem(z + flow_step(f), zs) * xs

    def steps_of_flows(f):
        near = jnp.where(f // 2 == 0, 0, zs // 2 - f // 2)
        return jnp.where(f % 2 == 0, near, jnp.where(near == 0, zs // 2, zs - near))

    def load(k, src, dst):
        return pltpu.make_async_copy(src, dst, load_sems.at[k])

    loads = [
        load(0, dec_hbm, dec),
        load(1, rows_hbm, rows),
        load(2, down_hbm, down),
        load(3, grad_hbm, grad),
        load(4, up_hbm, up),
        load(5, dec_index_hbm, dec_index_ref),
        load(6, store_hbm, store_ref),
        load(7, store_flat_hbm, store_s_ref),
        load(8, blk_hbm, blk_s_ref),
        load(9, live_hbm, live_s_ref),
    ]
    loads = loads[:1] + loads[5:] + loads[1:5]
    for one in loads:
        one.start()

    barrier = pltpu.get_barrier_semaphore()

    def greet(f, first):
        base = z_row(f)
        for dx in range(first, xs):
            pl.semaphore_signal(
                barrier, inc=1, device_id=(base + x_at[dx], t), device_id_type=MESH
            )

    def greet_flow(f, carry):
        greet(f, 0)
        return carry

    greet(0, 1)
    lax.fori_loop(1, zs, greet_flow, 0)

    for j in range(1, ts):
        pl.semaphore_signal(barrier, inc=1, device_id=(me, t_at[j]), device_id_type=MESH)

    for one in loads[1:6]:
        one.wait()

    adapters = store_ref.shape[1]
    hits = (iota((adapters, count), 0) == dec_index_ref[...]).astype(F32).astype(BF16)
    table = jnp.broadcast_to(store_ref[...], (8, adapters)).astype(F32).astype(BF16)
    slot = nn_dot(table, hits)[0:1].astype(I32)
    owner, local = slot // 2, slot % 2
    dz = (owner // xs - z + zs) % zs
    dx = (owner % xs - x + xs) % xs
    half = (dz >= zs // 2).astype(I32)
    k = jnp.where(dz < zs // 2, dz, jnp.where(dz == zs // 2, 0, zs - dz))
    turn = jnp.where(k == 0, 0, zs // 2 - k)
    block = turn * wide + half * xs + dx
    square = (count, count)
    block_rows = jnp.broadcast_to(block, square)
    block_cols = jnp.transpose(block_rows.astype(F32)).astype(I32)
    same = jnp.logical_and(block_rows == block_cols, iota(square, 0) < iota(square, 1))
    before = jnp.sum(same.astype(F32), axis=0, keepdims=True).astype(I32)
    place = block * BLOCK + before
    code = jnp.broadcast_to(place * 2 + local, square)
    code_cols = jnp.transpose(code.astype(F32)).astype(I32)
    place_cols = code_cols // 2
    named = (code_cols % 2 + 1).astype(F32)
    lanes = iota((count, 128), 1)
    slot_cols = jnp.broadcast_to(place_cols[:, 0:1] % BLOCK, (count, 128))
    spread = jnp.where(
        lanes % DEPTH == slot_cols, jnp.broadcast_to(named[:, 0:1], (count, 128)), 0.0
    )
    in_block = (iota((owners, count), 0) == block).astype(F32).astype(BF16)
    meta2[...] = nn_dot(in_block, spread.astype(BF16))

    def lift(i, carry):
        meta_send[i] = meta2[pl.ds(i, 1), :]
        return carry

    lax.fori_loop(0, owners, lift, 0)
    meta_got[0] = meta2[0:1, :]

    loads[0].wait()
    pl.semaphore_wait(barrier, owners - 1 + ts - 1)

    def start_rows(g, first):
        for half in range(2):
            base = z_row(2 * g + half)
            for dx in range(first if half == 0 else 0, xs):
                i = g * wide + half * xs + dx
                at = pl.ds(pl.multiple_of(i * BLOCK, BLOCK), BLOCK)
                to = dict(device_id=(base + x_at[dx], t), device_id_type=MESH)
                pltpu.make_async_remote_copy(
                    src_ref=send.at[at],
                    dst_ref=got.at[at],
                    send_sem=send_sem,
                    recv_sem=got_sems.at[g],
                    **to,
                ).start()
                pltpu.make_async_remote_copy(
                    src_ref=meta_send.at[i],
                    dst_ref=meta_got.at[i],
                    send_sem=meta_send_sem,
                    recv_sem=meta_got_sems.at[g],
                    **to,
                ).start()

    def dispatch(g):
        base = pl.multiple_of(g * gr, gr)
        rel = iota((gr, count), 0) + base
        sum_rows = jnp.zeros((gr, wc), F32)
        for c in range(CHUNKS):
            chosen = (rel == place + c * DEPTH).astype(F32).astype(BF16)
            sum_rows += nn_dot(chosen, dec[:, c * wc : (c + 1) * wc])
        send[pl.ds(base, gr), :] = sum_rows.astype(BF16)

    dispatch(0)
    start_rows(0, 1)
    got[0:BLOCK, :] = send[0:BLOCK, :]

    def dispatch_more(g, carry):
        dispatch(g)
        start_rows(g, 0)
        return carry

    dispatch_more(1, 0)

    step = dz
    flow = block // xs
    earlier = jnp.logical_or(
        block_cols < block_rows,
        jnp.logical_and(block_cols == block_rows, iota(square, 0) < iota(square, 1)),
    )
    mates = jnp.logical_and(block_cols // xs == block_rows // xs, earlier)
    queue = jnp.sum(mates.astype(F32), axis=0, keepdims=True).astype(I32)
    more = jnp.transpose(jnp.broadcast_to(step * 8 + before, square).astype(F32)).astype(I32)
    step_col, slot_col = more[:, 0:1] // 8, more[:, 0:1] % 8
    ring = iota((count, 128), 1) % zs
    load_of = jnp.sum((ring == step_col).astype(F32), axis=0, keepdims=True)

    def from_next(v):
        return pltpu.roll(v, 127, 1)

    def from_last(v):
        return pltpu.roll(v, 1, 1)

    load_of = jnp.broadcast_to(load_of, (8, 128))
    above, below = from_next(load_of), from_last(load_of)
    rest = jnp.maximum(load_of - KEPT, 0.0)
    moved = []
    for way, top in MOVES:
        can = ((above if way > 0 else below) <= top).astype(F32)
        if len(moved) == 2:
            can = can * (1.0 - from_last(from_last(moved[0])))
        if len(moved) == 3:
            can = can * (1.0 - from_next(from_next(moved[1])))
        now = jnp.where(rest > 0, can, 0.0)
        rest = rest - now
        moved.append(now)
    stuck = jnp.max(rest, axis=1, keepdims=True)
    row8 = iota((8, 128), 0)
    leave = jnp.zeros((8, 128), F32)
    enter = jnp.zeros((8, 128), F32)
    for m, (way, _) in enumerate(MOVES):
        leave = jnp.where(row8 == m, moved[m], leave)
        enter = jnp.where(row8 == m, from_last(moved[m]) if way > 0 else from_next(moved[m]), enter)
    at_step = (iota((128, count), 0) == step).astype(F32).astype(BF16)
    mine = nn_dot(leave.astype(BF16), at_step)
    code = jnp.where(queue < KEPT, queue + 1, 0)
    home_step, home_slot = step, queue
    seen = jnp.zeros((1, count), F32)
    over = (queue - KEPT).astype(F32)
    for m, (way, top) in enumerate(MOVES):
        used = mine[m : m + 1]
        hit = jnp.where(over == seen, used, 0.0) > 0.5
        code = jnp.where(hit, KEPT + 1 + m, code)
        home_step = jnp.where(hit, (step + zs + way) % zs, home_step)
        home_slot = jnp.where(hit, top, home_slot)
        seen = seen + used
    home_far = (home_step >= zs // 2).astype(I32)
    home_k = jnp.where(
        home_step < zs // 2, home_step, jnp.where(home_step == zs // 2, 0, zs - home_step)
    )
    home_turn = jnp.where(home_k == 0, 0, zs // 2 - home_k)
    home = jnp.where(code > 0, (2 * home_turn + home_far) * 16 + home_slot, 4095)
    home_cols = jnp.transpose(jnp.broadcast_to(home, square).astype(F32)).astype(I32)[:, 0:1]
    code_col = jnp.transpose(jnp.broadcast_to(code, square).astype(F32))[:, 0:1]
    block_col = block_cols[:, 0:1]
    lane_x = lanes // BLOCK
    lane_r = lanes % DEPTH
    fits = jnp.logical_and(lane_x == block_col % xs, lane_r == slot_col)
    codes = jnp.where(fits, jnp.broadcast_to(code_col, (count, 128)), 0.0).astype(BF16)
    in_flow = (iota((zs, count), 0) == flow).astype(F32).astype(BF16)
    signs = jnp.concatenate(
        [
            jnp.zeros((64, 128), F32),
            leave,
            enter,
            jnp.broadcast_to(stuck, (8, 128)),
            jnp.zeros((40, 128), F32),
        ],
        axis=0,
    )
    signs = jnp.transpose(signs).astype(BF16)
    fi = iota((zs, 128), 0)
    f_step = steps_of_flows(fi)
    pick = (f_step == iota((zs, 128), 1)).astype(F32).astype(BF16)
    rmeta2[...] = nn_dot(in_flow, codes) + nn_dot(pick, signs)

    def lift_plan(f, carry):
        rmeta_send[f] = rmeta2[pl.ds(f, 1), :]
        return carry

    lax.fori_loop(0, zs, lift_plan, 0)
    rmeta_got[0] = rmeta2[0:1, :]

    def start_plan(f, carry):
        pltpu.make_async_remote_copy(
            src_ref=rmeta_send.at[f],
            dst_ref=rmeta_got.at[f],
            send_sem=rmeta_send_sem,
            recv_sem=rmeta_got_sem,
            device_id=(z_peer(flow_step(f)), t),
            device_id_type=MESH,
        ).start()
        return carry

    lax.fori_loop(1, zs, start_plan, 0)

    lax.fori_loop(2, groups, dispatch_more, 0)

    rank = down.shape[0] // 2
    learn = rows.shape[0]
    own_slot = store_s_ref[blk_s_ref[0]] % 2
    aj = iota((learn, 2 * rank), 1)
    own = (aj // rank == own_slot).astype(F32)
    loads[6].wait()
    loads[7].wait()
    forward = nt_dot(rows[...], down[...]) * own
    loads[8].wait()
    loads[9].wait()
    backward = nt_dot(grad[...], up[...]) * own
    forward = forward + pltpu.roll(forward, rank, 1)
    backward = backward + pltpu.roll(backward, rank, 1)
    lpart[...] = jnp.where(aj < rank, forward, backward)

    def lpart_copy(j):
        return pltpu.make_async_remote_copy(
            src_ref=lpart,
            dst_ref=lpart_got.at[j - 1],
            send_sem=lpart_send_sem,
            recv_sem=lpart_got_sem,
            device_id=(me, t_at[j]),
            device_id_type=MESH,
        )

    for j in range(1, ts):
        lpart_copy(j).start()

    def wait_group(g, ref, size, sems):
        @pl.when(g == 0)
        def _():
            view = ref.at[pl.ds(size, (wide - 1) * size)]
            pltpu.make_async_copy(view, view, sems.at[g]).wait()

        @pl.when(g > 0)
        def _():
            view = ref.at[pl.ds(pl.multiple_of(g * wide * size, wide * size), wide * size)]
            pltpu.make_async_copy(view, view, sems.at[g]).wait()

    chunk_of = (iota((gr, 2 * rank), 0) % BLOCK) // DEPTH
    lane = iota((gr, 2 * rank), 1)

    def chosen_mask(g):
        ids = meta_got[pl.ds(g * wide, wide)]
        ids = jnp.broadcast_to(ids, (wide, BLOCK, 128)).reshape(gr, 128)
        mine = iota((gr, 128), 1) == iota((gr, 128), 0) % DEPTH
        which = jnp.sum(jnp.where(mine, ids, 0.0), axis=1, keepdims=True)
        return (which == (lane // rank + 1).astype(F32)).astype(F32)

    pairs = wide // 2
    top3 = iota((wide, 8, 2 * rank), 1) < DEPTH
    left3 = iota((wide, 8, 2 * rank), 2) < rank

    def part_copy(g, j):
        return pltpu.make_async_remote_copy(
            src_ref=part.at[g],
            dst_ref=part_got.at[g, j - 1],
            send_sem=part_send_sem,
            recv_sem=part_got_sems.at[g],
            device_id=(me, t_at[j]),
            device_id_type=MESH,
        )

    def ranks(g):
        wait_group(g, got, BLOCK, got_sems)
        wait_group(g, meta_got, 1, meta_got_sems)
        at = pl.ds(pl.multiple_of(g * gr, gr), gr)
        block_rows = got[at, :]
        both = jnp.zeros((gr, 2 * rank), F32)
        for c in range(CHUNKS):
            one = nt_dot(block_rows, down[:, c * wc : (c + 1) * wc])
            both = both + jnp.where(chunk_of == c, one, 0.0)
        both = both * chosen_mask(g)
        both = both.reshape(wide, 2, 8, 2 * rank)
        both = both[:, 0] + both[:, 1]
        both = both + pltpu.roll(both, DEPTH, 1)
        both = both + pltpu.roll(both, rank, 2)
        both = both.reshape(2, pairs, 8, 2 * rank)
        two = jnp.where(top3[:pairs], both[0], both[1])
        two = two.reshape(2, pairs // 2, 8, 2 * rank)
        part[g] = jnp.where(left3[: pairs // 2], two[0], two[1])

        for j in range(1, ts):
            part_copy(g, j).start()

    def start_cross(g):
        for half in range(2):
            for dx in range(xs):
                row = (g * wide + half * xs + dx) * BLOCK
                at = pl.ds(pl.multiple_of(row, BLOCK), BLOCK)
                if dx == 0:
                    pltpu.make_async_copy(dsend.at[at], xgot.at[at], xgot_sems.at[g]).start()
                else:
                    pltpu.make_async_remote_copy(
                        src_ref=dsend.at[at],
                        dst_ref=xgot.at[at],
                        send_sem=xsend_sem,
                        recv_sem=xgot_sems.at[g],
                        device_id=(x_peer(xs - dx), t),
                        device_id_type=MESH,
                    ).start()

    def deltas(g):
        view = part_got.at[g]
        pltpu.make_async_copy(view, view, part_got_sems.at[g]).wait()
        v = part[g]
        for j in range(ts - 1):
            v = v + part_got[g, j]
        v = (v * shrink).astype(BF16).astype(F32)
        turned = pltpu.roll(v, rank, 2)
        keep = left3[: pairs // 2]
        two = jnp.concatenate([jnp.where(keep, v, turned), jnp.where(keep, turned, v)], axis=0)
        turned = pltpu.roll(two, DEPTH, 1)
        keep = top3[:pairs]
        both = jnp.concatenate([jnp.where(keep, two, turned), jnp.where(keep, turned, two)], axis=0)
        both = jnp.broadcast_to(both[:, None], (wide, 2, 8, 2 * rank)).reshape(gr, 2 * rank)
        both = both * chosen_mask(g)
        base = pl.multiple_of(g * gr, gr)
        sum_rows = jnp.zeros((gr, hc), F32)
        for c in range(CHUNKS):
            left = jnp.where(chunk_of == c, both, 0.0).astype(BF16)
            sum_rows += nn_dot(left, up[:, c * hc : (c + 1) * hc])
        dsend[pl.ds(base, gr), :] = (sum_rows * expand).astype(BF16)

        start_cross(g)

    def read_plans():
        view = rmeta_got.at[pl.ds(1, zs - 1)]
        pltpu.make_async_copy(view, view, rmeta_got_sem).wait()
        plan = rmeta_got[...].reshape(zs, 128)
        lane16 = iota((zs, 128), 1)
        source = (z + zs - f_step) % zs
        other_f = iota((zs, zs), 1)
        other_step = steps_of_flows(other_f)
        other = (z + zs - other_step) % zs
        first = (other < source[:, 0:1]).astype(F32).astype(BF16)
        ahead = nn_dot(first, plan.astype(BF16))

        def column(v, n):
            return jnp.sum(jnp.where(lane16 == n, v, 0.0), axis=1, keepdims=True)

        def places(base, order):
            here = [column(plan, base + m) for m in order]
            at = column(ahead, base + order[0])
            for m in order[1:]:
                at = at + column(ahead, base + m)
            out = []
            for one in here:
                out.append(jnp.where(one > 0.5, at, -1.0))
                at = at + one
            return out, at

        ups = [m for m, (way, _) in enumerate(MOVES) if way > 0]
        downs = [m for m, (way, _) in enumerate(MOVES) if way < 0]
        t_slot[...] = jnp.where(plan < KEPT + 0.5, plan - 1.0, -1.0)
        worst = column(plan, 80)
        for table, order in ((t_plus, ups), (t_minus, downs)):
            spots, end = places(64, order)
            worst = jnp.maximum(worst, jnp.where(end > SPARE + 0.5, 1.0, 0.0))
            value = jnp.full((zs, 128), -1.0, F32)
            for m, spot in zip(order, spots):
                value = jnp.where(plan == KEPT + 1.0 + m, spot, value)
            table[...] = value
        value = jnp.full((zs, 128), -1.0, F32)
        spot_lane = (lane16 % SPARE).astype(F32)
        side_lane = lane16 // (SPARE * CHUNKS)
        for side, order in ((0, ups), (1, downs)):
            spots, _ = places(72, order)
            for m, spot in zip(order, spots):
                hit = jnp.logical_and(side_lane == side, spot_lane == spot)
                value = jnp.where(hit, MOVES[m][1] - 8.0, value)
        t_in[...] = value
        worst = jnp.max(worst, axis=0, keepdims=True)
        flag_send[...] = jnp.broadcast_to(worst, (1, 128))
        flag_got[0] = flag_send[...]

        def start(f, carry):
            pltpu.make_async_remote_copy(
                src_ref=flag_send,
                dst_ref=flag_got.at[f],
                send_sem=flag_sems.at[0],
                recv_sem=flag_sems.at[1],
                device_id=(z_peer(flow_step(f)), t),
                device_id_type=MESH,
            ).start()
            return carry

        lax.fori_loop(1, zs, start, 0)
        spill[...] = jnp.zeros_like(spill)

    def pick_rows(table, f, per, cells):
        shape = (per * CHUNKS, cells)
        wanted = (iota(shape, 0) % per).astype(F32)
        here = jnp.broadcast_to(table[pl.ds(f, 1), :][:, :cells], shape)
        return here, wanted, iota(shape, 0) // per

    cells = xs * BLOCK
    kept_a, kept_b = 8 * CHUNKS, DEPTH * CHUNKS

    def a_copy(f):
        at = pl.ds(pl.multiple_of(f * kept_a, kept_a), kept_a)
        return pltpu.make_async_remote_copy(
            src_ref=asend.at[at],
            dst_ref=agot.at[at],
            send_sem=asend_sem,
            recv_sem=agot_sems.at[lax.div(f, 2)],
            device_id=(z_peer(zs - flow_step(f)), t),
            device_id_type=MESH,
        )

    def start_a(f, carry):
        a_copy(f).start()
        return carry

    held_back = min(3, groups - 1)

    def relay(g):
        view = xgot.at[pl.ds(pl.multiple_of(g * gr, gr), gr)]
        pltpu.make_async_copy(view, view, xgot_sems.at[g]).wait()

        def one_flow(f, carry):
            chunk = (iota((1, cells), 1) % BLOCK) // DEPTH
            picks = []
            for table, per, base in (
                (t_slot, 8, 0.0),
                (t_slot, DEPTH, 8.0),
                (t_plus, SPARE, 0.0),
                (t_minus, SPARE, 0.0),
            ):
                here, wanted, c = pick_rows(table, f, per, cells)
                hit = jnp.logical_and(here == wanted + base, chunk == c)
                picks.append(hit.astype(F32))
            picks = jnp.concatenate(picks, axis=0).astype(BF16)
            blocks = xgot[pl.ds(pl.multiple_of(f * cells, cells), cells), :]
            packed = nn_dot(picks, blocks)
            asend[pl.ds(pl.multiple_of(f * kept_a, kept_a), kept_a), :] = packed[:kept_a].astype(BF16)
            bsend[pl.ds(pl.multiple_of(f * kept_b, kept_b), kept_b), :] = packed[
                kept_a : kept_a + kept_b
            ].astype(BF16)
            spill[...] += packed[kept_a + kept_b :]
            return carry

        lax.fori_loop(2 * g, 2 * g + 2, one_flow, 0)

        @pl.when(g == 0)
        def _():
            agot[0:kept_a, :] = asend[0:kept_a, :]
            lax.fori_loop(1, 2, start_a, 0)

        @pl.when(jnp.logical_and(g > 0, g < groups - held_back))
        def _():
            lax.fori_loop(2 * g, 2 * g + 2, start_a, 0)

    def stage(s, carry):
        @pl.when(s == 2)
        def _():
            read_plans()

        @pl.when(jnp.logical_and(s >= 2, s < groups + 2))
        def _():
            deltas(s - 2)

        @pl.when(s >= 3)
        def _():
            relay(s - 3)

        @pl.when(s < groups)
        def _():
            ranks(s)

        return carry

    lax.fori_loop(0, groups + 3, stage, 0)

    spare = SPARE * CHUNKS
    fsend[...] = spill[...].astype(BF16)
    for side, way in ((0, 1), (1, zs - 1)):
        at = pl.ds(side * spare, spare)
        pltpu.make_async_remote_copy(
            src_ref=fsend.at[at],
            dst_ref=fgot.at[at],
            send_sem=fsend_sem,
            recv_sem=fgot_sem,
            device_id=(z_peer(way), t),
            device_id_type=MESH,
        ).start()
    lax.fori_loop(2 * (groups - held_back), 2 * groups, start_a, 0)

    pltpu.make_async_copy(lpart_got, lpart_got, lpart_got_sem).wait()
    v = lpart[...]
    for j in range(ts - 1):
        v = v + lpart_got[j]
    live = (iota((learn, 2 * rank), 0) < live_s_ref[0]).astype(F32)
    scale = jnp.where(aj < rank, shrink, expand)
    v = (v * scale * live).astype(BF16).astype(F32)
    turned = pltpu.roll(v, rank, 1)
    act = (jnp.where(aj < rank, v, turned) * own).astype(BF16)
    back = (jnp.where(aj < rank, turned, v) * own).astype(BF16)
    for c in range(CHUNKS):
        at = slice(c * wc, (c + 1) * wc)
        g_a = tn_dot(back, rows[:, at]) * shrink
        down_out[:, at] = (down[:, at].astype(F32) - DOWN_RATE * g_a).astype(BF16)
    for c in range(CHUNKS):
        at = slice(c * hc, (c + 1) * hc)
        g_b = tn_dot(act, grad[:, at]) * expand
        up_out[:, at] = (up[:, at].astype(F32) - UP_RATE * g_b).astype(BF16)

    pltpu.make_async_copy(fgot, fgot, fgot_sem).wait()

    def b_copy(f):
        at = pl.ds(pl.multiple_of(f * kept_b, kept_b), kept_b)
        return pltpu.make_async_remote_copy(
            src_ref=bsend.at[at],
            dst_ref=bgot.at[at],
            send_sem=bsend_sem,
            recv_sem=bgot_sems.at[lax.div(f, 4)],
            device_id=(z_peer(zs - flow_step(f)), t),
            device_id_type=MESH,
        )

    def finish_b(f, carry):
        here, wanted, c = pick_rows(t_in, f, DEPTH, 2 * spare)
        chunk = (iota((1, 2 * spare), 1) % spare) // SPARE
        hit = jnp.logical_and(here == wanted, chunk == c)
        at = pl.ds(pl.multiple_of(f * kept_b, kept_b), kept_b)
        extra = nn_dot(hit.astype(F32).astype(BF16), fgot[...])
        bsend[at, :] = (bsend[at, :].astype(F32) + extra).astype(BF16)

        @pl.when(f > 0)
        def _():
            b_copy(f).start()

        return carry

    lax.fori_loop(0, zs, finish_b, 0)
    bgot[0:kept_b, :] = bsend[0:kept_b, :]

    pltpu.make_async_copy(
        flag_got.at[pl.ds(1, zs - 1)], flag_got.at[pl.ds(1, zs - 1)], flag_sems.at[1]
    ).wait()
    worst = flag_got[0]
    for f in range(1, zs):
        worst = jnp.maximum(worst, flag_got[f])
    flagx_send[...] = worst
    for dx in range(1, xs):
        pltpu.make_async_remote_copy(
            src_ref=flagx_send,
            dst_ref=flagx_got.at[dx - 1],
            send_sem=flag_sems.at[2],
            recv_sem=flag_sems.at[3],
            device_id=(x_peer(dx), t),
            device_id_type=MESH,
        ).start()

    total[...] = jnp.zeros_like(total)
    pair = 2 * kept_a
    home_flow = jnp.broadcast_to(home_cols // 16, (count, pair))
    home_slot = jnp.broadcast_to(home_cols % 16, (count, pair))
    in_a = home_slot < 8
    place_a = jnp.where(in_a, home_flow * kept_a + home_slot, -4096)
    place_b = jnp.where(in_a, -4096, home_flow * kept_b + home_slot - 8)

    def add_up(ref, g, place, chunk_rows):
        base = pl.multiple_of(g * pair, pair)
        rel = iota((count, pair), 1) + base
        arrived = ref[pl.ds(base, pair), :]
        for c in range(CHUNKS):
            chosen = (rel == place + c * chunk_rows).astype(F32).astype(BF16)
            total[:, c * hc : (c + 1) * hc] += nn_dot(chosen, arrived)

    def wait_pair(ref, g, own, sems):
        @pl.when(g == 0)
        def _():
            view = ref.at[pl.ds(own, pair - own)]
            pltpu.make_async_copy(view, view, sems.at[g]).wait()

        @pl.when(g > 0)
        def _():
            view = ref.at[pl.ds(pl.multiple_of(g * pair, pair), pair)]
            pltpu.make_async_copy(view, view, sems.at[g]).wait()

    def combine_a(g, carry):
        wait_pair(agot, g, kept_a, agot_sems)
        add_up(agot, g, place_a, 8)
        return carry

    lax.fori_loop(0, groups, combine_a, 0)

    def combine_b(g, carry):
        wait_pair(bgot, g, kept_b, bgot_sems)
        add_up(bgot, g, place_b, DEPTH)
        return carry

    lax.fori_loop(0, zs // 4, combine_b, 0)
    delta_out[...] = total[...].astype(BF16)
    pltpu.make_async_copy(flagx_got, flagx_got, flag_sems.at[3]).wait()
    worst = flagx_send[...]
    for dx in range(1, xs):
        worst = jnp.maximum(worst, flagx_got[dx - 1])
    flag_out[0] = jnp.max(worst).astype(I32)

    def drain(view, sem):
        pltpu.make_async_copy(view, view, sem).wait()

    drain(send.at[pl.ds(BLOCK, (owners - 1) * BLOCK)], send_sem)
    drain(meta_send.at[pl.ds(1, owners - 1)], meta_send_sem)
    drain(dsend.at[pl.ds(0, zs * (xs - 1) * BLOCK)], xsend_sem)
    drain(rmeta_send.at[pl.ds(1, zs - 1)], rmeta_send_sem)
    drain(asend.at[pl.ds(kept_a, (zs - 1) * kept_a)], asend_sem)
    drain(bsend.at[pl.ds(kept_b, (zs - 1) * kept_b)], bsend_sem)
    drain(fsend, fsend_sem)
    drain(flag_got.at[pl.ds(1, zs - 1)], flag_sems.at[0])
    drain(flagx_got, flag_sems.at[2])
    drain(lpart_got, lpart_send_sem)
    drain(part_got, part_send_sem)


def padded_kernel(
    geometry,
    dec_hbm,
    dec_index_hbm,
    store_hbm,
    down_hbm,
    up_hbm,
    delta_out,
    dec_index_ref,
    store_ref,
    dec,
    down,
    up,
    send,
    got,
    meta2,
    meta_send,
    meta_got,
    part,
    part_got,
    dsend,
    dgot,
    total,
    load_sems,
    send_sem,
    got_sems,
    meta_send_sem,
    meta_got_sems,
    part_send_sem,
    part_got_sems,
    dsend_sem,
    dgot_sems,
):
    zs, xs, ts, shrink, expand = geometry
    owners = zs * xs
    wide = 2 * xs
    groups = zs // 2
    gr = wide * BLOCK
    me = lax.axis_index("dp")
    t = lax.axis_index("tensor")
    z, x = me // xs, me % xs
    count = dec.shape[0]
    wc = dec.shape[1] // CHUNKS
    hc = up.shape[1] // CHUNKS

    def offset(i):
        k = (zs // 2 - i // wide) % (zs // 2)
        half = (i % wide) // xs
        dz = k + half * (zs - 2 * k - (zs // 2) * ((zs - k) // zs))
        return dz, i % xs

    def owner_of(i):
        dz, dx = offset(i)
        return ((z + dz) % zs) * xs + (x + dx) % xs

    def source_of(i):
        dz, dx = offset(i)
        return ((z + zs - dz) % zs) * xs + (x + xs - dx) % xs

    def load(k, src, dst):
        return pltpu.make_async_copy(src, dst, load_sems.at[k])

    loads = [
        load(0, dec_hbm, dec),
        load(1, dec_index_hbm, dec_index_ref),
        load(2, store_hbm, store_ref),
        load(3, down_hbm, down),
        load(4, up_hbm, up),
    ]
    for one in loads:
        one.start()

    barrier = pltpu.get_barrier_semaphore()

    def greet(i, carry):
        pl.semaphore_signal(barrier, inc=1, device_id=(owner_of(i), t), device_id_type=MESH)
        return carry

    lax.fori_loop(1, owners, greet, 0)

    def greet_t(j, carry):
        pl.semaphore_signal(barrier, inc=1, device_id=(me, (t + j) % ts), device_id_type=MESH)
        return carry

    lax.fori_loop(1, ts, greet_t, 0)

    for one in loads[1:3]:
        one.wait()

    adapters = store_ref.shape[1]
    hits = (iota((adapters, count), 0) == dec_index_ref[...]).astype(F32).astype(BF16)
    table = jnp.broadcast_to(store_ref[...], (8, adapters)).astype(F32).astype(BF16)
    slot = nn_dot(table, hits)[0:1].astype(I32)
    owner, local = slot // 2, slot % 2
    dz = (owner // xs - z + zs) % zs
    dx = (owner % xs - x + xs) % xs
    half = (dz >= zs // 2).astype(I32)
    k = jnp.where(dz < zs // 2, dz, jnp.where(dz == zs // 2, 0, zs - dz))
    turn = jnp.where(k == 0, 0, zs // 2 - k)
    block = turn * wide + half * xs + dx
    square = (count, count)
    block_rows = jnp.broadcast_to(block, square)
    block_cols = jnp.transpose(block_rows.astype(F32)).astype(I32)
    same = jnp.logical_and(block_rows == block_cols, iota(square, 0) < iota(square, 1))
    before = jnp.sum(same.astype(F32), axis=0, keepdims=True).astype(I32)
    place = block * BLOCK + before
    code = jnp.broadcast_to(place * 2 + local, square)
    code_cols = jnp.transpose(code.astype(F32)).astype(I32)
    place_cols = code_cols // 2
    named = (code_cols % 2 + 1).astype(F32)
    lanes = iota((count, 128), 1)
    slot_cols = jnp.broadcast_to(place_cols[:, 0:1] % BLOCK, (count, 128))
    spread = jnp.where(
        lanes % DEPTH == slot_cols, jnp.broadcast_to(named[:, 0:1], (count, 128)), 0.0
    )
    in_block = (iota((owners, count), 0) == block).astype(F32).astype(BF16)
    meta2[...] = nn_dot(in_block, spread.astype(BF16))

    def lift(i, carry):
        meta_send[i] = meta2[pl.ds(i, 1), :]
        return carry

    lax.fori_loop(0, owners, lift, 0)
    meta_got[0] = meta2[0:1, :]

    loads[0].wait()
    pl.semaphore_wait(barrier, owners - 1 + ts - 1)

    def row_copy(i):
        at = pl.ds(pl.multiple_of(i * BLOCK, BLOCK), BLOCK)
        return pltpu.make_async_remote_copy(
            src_ref=send.at[at],
            dst_ref=got.at[at],
            send_sem=send_sem,
            recv_sem=got_sems.at[i // wide],
            device_id=(owner_of(i), t),
            device_id_type=MESH,
        )

    def meta_copy(i):
        return pltpu.make_async_remote_copy(
            src_ref=meta_send.at[i],
            dst_ref=meta_got.at[i],
            send_sem=meta_send_sem,
            recv_sem=meta_got_sems.at[i // wide],
            device_id=(owner_of(i), t),
            device_id_type=MESH,
        )

    def start_rows(i, carry):
        meta_copy(i).start()
        row_copy(i).start()
        return carry

    def dispatch(g):
        base = pl.multiple_of(g * gr, gr)
        rel = iota((gr, count), 0) + base
        sum_rows = jnp.zeros((gr, wc), F32)
        for c in range(CHUNKS):
            chosen = (rel == place + c * DEPTH).astype(F32).astype(BF16)
            sum_rows += nn_dot(chosen, dec[:, c * wc : (c + 1) * wc])
        send[pl.ds(base, gr), :] = sum_rows.astype(BF16)

    dispatch(0)
    lax.fori_loop(1, wide, start_rows, 0)
    got[0:BLOCK, :] = send[0:BLOCK, :]

    def dispatch_more(g, carry):
        dispatch(g)
        lax.fori_loop(g * wide, (g + 1) * wide, start_rows, 0)
        return carry

    lax.fori_loop(1, groups, dispatch_more, 0)

    rank = down.shape[0] // 2
    loads[3].wait()
    loads[4].wait()

    def wait_group(g, ref, size, sems):
        @pl.when(g == 0)
        def _():
            view = ref.at[pl.ds(size, (wide - 1) * size)]
            pltpu.make_async_copy(view, view, sems.at[g]).wait()

        @pl.when(g > 0)
        def _():
            view = ref.at[pl.ds(pl.multiple_of(g * wide * size, wide * size), wide * size)]
            pltpu.make_async_copy(view, view, sems.at[g]).wait()

    chunk_of = (iota((gr, 2 * rank), 0) % BLOCK) // DEPTH
    lane = iota((gr, 2 * rank), 1)

    def chosen_mask(g):
        ids = meta_got[pl.ds(g * wide, wide)]
        ids = jnp.broadcast_to(ids, (wide, BLOCK, 128)).reshape(gr, 128)
        mine = iota((gr, 128), 1) == iota((gr, 128), 0) % DEPTH
        which = jnp.sum(jnp.where(mine, ids, 0.0), axis=1, keepdims=True)
        return (which == (lane // rank + 1).astype(F32)).astype(F32)

    pairs = wide // 2
    top3 = iota((wide, 8, 2 * rank), 1) < DEPTH
    left3 = iota((wide, 8, 2 * rank), 2) < rank

    def part_copy(g, j):
        return pltpu.make_async_remote_copy(
            src_ref=part.at[g],
            dst_ref=part_got.at[g, j - 1],
            send_sem=part_send_sem,
            recv_sem=part_got_sems.at[g],
            device_id=(me, (t + j) % ts),
            device_id_type=MESH,
        )

    def ranks(g):
        wait_group(g, got, BLOCK, got_sems)
        wait_group(g, meta_got, 1, meta_got_sems)
        at = pl.ds(pl.multiple_of(g * gr, gr), gr)
        block_rows = got[at, :]
        both = jnp.zeros((gr, 2 * rank), F32)
        for c in range(CHUNKS):
            one = nt_dot(block_rows, down[:, c * wc : (c + 1) * wc])
            both = both + jnp.where(chunk_of == c, one, 0.0)
        both = both * chosen_mask(g)
        both = both.reshape(wide, 2, 8, 2 * rank)
        both = both[:, 0] + both[:, 1]
        both = both + pltpu.roll(both, DEPTH, 1)
        both = both + pltpu.roll(both, rank, 2)
        both = both.reshape(2, pairs, 8, 2 * rank)
        two = jnp.where(top3[:pairs], both[0], both[1])
        two = two.reshape(2, pairs // 2, 8, 2 * rank)
        part[g] = jnp.where(left3[: pairs // 2], two[0], two[1])

        def start(j, carry):
            part_copy(g, j).start()
            return carry

        lax.fori_loop(1, ts, start, 0)

    def delta_copy(i):
        at = pl.ds(pl.multiple_of(i * BLOCK, BLOCK), BLOCK)
        return pltpu.make_async_remote_copy(
            src_ref=dsend.at[at],
            dst_ref=dgot.at[at],
            send_sem=dsend_sem,
            recv_sem=dgot_sems.at[i // wide],
            device_id=(source_of(i), t),
            device_id_type=MESH,
        )

    def start_delta(i, carry):
        delta_copy(i).start()
        return carry

    def deltas(g):
        view = part_got.at[g]
        pltpu.make_async_copy(view, view, part_got_sems.at[g]).wait()
        v = part[g]
        for j in range(ts - 1):
            v = v + part_got[g, j]
        v = (v * shrink).astype(BF16).astype(F32)
        turned = pltpu.roll(v, rank, 2)
        keep = left3[: pairs // 2]
        two = jnp.concatenate([jnp.where(keep, v, turned), jnp.where(keep, turned, v)], axis=0)
        turned = pltpu.roll(two, DEPTH, 1)
        keep = top3[:pairs]
        both = jnp.concatenate([jnp.where(keep, two, turned), jnp.where(keep, turned, two)], axis=0)
        both = jnp.broadcast_to(both[:, None], (wide, 2, 8, 2 * rank)).reshape(gr, 2 * rank)
        both = both * chosen_mask(g)
        base = pl.multiple_of(g * gr, gr)
        sum_rows = jnp.zeros((gr, hc), F32)
        for c in range(CHUNKS):
            left = jnp.where(chunk_of == c, both, 0.0).astype(BF16)
            sum_rows += nn_dot(left, up[:, c * hc : (c + 1) * hc])
        dsend[pl.ds(base, gr), :] = (sum_rows * expand).astype(BF16)

        @pl.when(g == 0)
        def _():
            dgot[0:BLOCK, :] = dsend[0:BLOCK, :]
            lax.fori_loop(1, wide, start_delta, 0)

        @pl.when(g > 0)
        def _():
            lax.fori_loop(g * wide, (g + 1) * wide, start_delta, 0)

    ranks(0)

    def step(g, carry):
        ranks(g)
        deltas(g - 1)
        return carry

    lax.fori_loop(1, groups, step, 0)
    deltas(groups - 1)

    total[...] = jnp.zeros_like(total)
    place_128 = jnp.broadcast_to(place_cols[:, 0:1], (count, gr))

    def combine(g, carry):
        wait_group(g, dgot, BLOCK, dgot_sems)
        base = pl.multiple_of(g * gr, gr)
        rel = iota((count, gr), 1) + base
        arrived = dgot[pl.ds(base, gr), :]
        for c in range(CHUNKS):
            chosen = (rel == place_128 + c * DEPTH).astype(F32).astype(BF16)
            total[:, c * hc : (c + 1) * hc] += nn_dot(chosen, arrived)
        return carry

    lax.fori_loop(0, groups, combine, 0)
    delta_out[...] = total[...].astype(BF16)

    def drain(view, sem):
        pltpu.make_async_copy(view, view, sem).wait()

    drain(send.at[pl.ds(BLOCK, (owners - 1) * BLOCK)], send_sem)
    drain(meta_send.at[pl.ds(1, owners - 1)], meta_send_sem)
    drain(dsend.at[pl.ds(BLOCK, (owners - 1) * BLOCK)], dsend_sem)
    drain(part_got, part_send_sem)


def padded_exchange(
    decode_input_rows,
    decode_adapter_index,
    adapter_storage_index,
    down_rows,
    up_rows,
):
    owners = lax.axis_size("dp")
    ts = lax.axis_size("tensor")
    xs = 4
    zs = owners // xs
    count, width = decode_input_rows.shape
    both, hidden = up_rows.shape
    groups = zs // 2
    wide = 2 * xs
    hbm = pl.BlockSpec(memory_space=pltpu.HBM)
    dma = pltpu.SemaphoreType.DMA
    packed = (wide // 4, 8, both)
    geometry = (zs, xs, ts, (width * ts) ** (-0.5), (both // 2) ** (-0.5))
    return pl.pallas_call(
        functools.partial(padded_kernel, geometry),
        out_shape=jax.ShapeDtypeStruct((count, hidden), BF16),
        in_specs=[hbm] * 5,
        out_specs=pl.BlockSpec(memory_space=pltpu.VMEM),
        scratch_shapes=[
            pltpu.VMEM((1, count), I32),
            pltpu.VMEM((1, adapter_storage_index.shape[0]), I32),
            pltpu.VMEM((count, width), BF16),
            pltpu.VMEM((both, width), BF16),
            pltpu.VMEM((both, hidden), BF16),
            pltpu.VMEM((owners * BLOCK, width // CHUNKS), BF16),
            pltpu.VMEM((owners * BLOCK, width // CHUNKS), BF16),
            pltpu.VMEM((owners, 128), F32),
            pltpu.VMEM((owners, 1, 128), F32),
            pltpu.VMEM((owners, 1, 128), F32),
            pltpu.VMEM((groups,) + packed, F32),
            pltpu.VMEM((groups, ts - 1) + packed, F32),
            pltpu.VMEM((owners * BLOCK, hidden // CHUNKS), BF16),
            pltpu.VMEM((owners * BLOCK, hidden // CHUNKS), BF16),
            pltpu.VMEM((count, hidden), F32),
            dma((5,)),
            dma,
            dma((groups,)),
            dma,
            dma((groups,)),
            dma,
            dma((groups,)),
            dma,
            dma((groups,)),
        ],
        compiler_params=pltpu.CompilerParams(
            collective_id=1, has_side_effects=True, vmem_limit_bytes=VMEM_LIMIT
        ),
    )(
        decode_input_rows,
        decode_adapter_index.reshape(1, count),
        adapter_storage_index.reshape(1, -1),
        down_rows,
        up_rows,
    )


def local(
    decode_input_rows,
    decode_adapter_index,
    adapter_storage_index,
    learner_input_rows,
    learner_gradient,
    block_adapter_index,
    block_live_count,
    adapter_down_weight,
    adapter_up_weight,
):
    owners = lax.axis_size("dp")
    ts = lax.axis_size("tensor")
    xs = 4
    zs = owners // xs
    held, rank, width = adapter_down_weight.shape
    hidden = adapter_up_weight.shape[2]
    count = decode_input_rows.shape[0]
    learn = learner_input_rows.shape[0]
    shrink = (width * ts) ** (-0.5)
    expand = rank ** (-0.5)
    groups = zs // 2
    wide = 2 * xs
    vmem = pl.BlockSpec(memory_space=pltpu.VMEM)
    hbm = pl.BlockSpec(memory_space=pltpu.HBM)
    dma = pltpu.SemaphoreType.DMA
    packed = (wide // 4, 8, 2 * rank)
    rows_a, rows_b, spare = 8 * CHUNKS, DEPTH * CHUNKS, SPARE * CHUNKS
    chunk = hidden // CHUNKS
    delta, down, up, flag = pl.pallas_call(
        functools.partial(kernel, (zs, xs, ts, shrink, expand)),
        out_shape=(
            jax.ShapeDtypeStruct((count, hidden), BF16),
            jax.ShapeDtypeStruct((held * rank, width), BF16),
            jax.ShapeDtypeStruct((held * rank, hidden), BF16),
            jax.ShapeDtypeStruct((1,), I32),
        ),
        in_specs=[hbm] * 10,
        out_specs=(vmem, vmem, vmem, pl.BlockSpec(memory_space=pltpu.SMEM)),
        scratch_shapes=[
            pltpu.VMEM((1, count), I32),
            pltpu.VMEM((1, adapter_storage_index.shape[0]), I32),
            pltpu.SMEM((adapter_storage_index.shape[0],), I32),
            pltpu.SMEM((1,), I32),
            pltpu.SMEM((1,), I32),
            pltpu.VMEM((count, width), BF16),
            pltpu.VMEM((learn, width), BF16),
            pltpu.VMEM((learn, hidden), BF16),
            pltpu.VMEM((held * rank, width), BF16),
            pltpu.VMEM((held * rank, hidden), BF16),
            pltpu.VMEM((owners * BLOCK, width // CHUNKS), BF16),
            pltpu.VMEM((owners * BLOCK, width // CHUNKS), BF16),
            pltpu.VMEM((owners, 128), F32),
            pltpu.VMEM((owners, 1, 128), F32),
            pltpu.VMEM((owners, 1, 128), F32),
            pltpu.VMEM((groups,) + packed, F32),
            pltpu.VMEM((groups, ts - 1) + packed, F32),
            pltpu.VMEM((learn, 2 * rank), F32),
            pltpu.VMEM((ts - 1, learn, 2 * rank), F32),
            pltpu.VMEM((owners * BLOCK, chunk), BF16),
            pltpu.VMEM((owners * BLOCK, chunk), BF16),
            pltpu.VMEM((zs, 128), F32),
            pltpu.VMEM((zs, 1, 128), F32),
            pltpu.VMEM((zs, 1, 128), F32),
            pltpu.VMEM((zs, 128), F32),
            pltpu.VMEM((zs, 128), F32),
            pltpu.VMEM((zs, 128), F32),
            pltpu.VMEM((zs, 128), F32),
            pltpu.VMEM((zs * rows_a, chunk), BF16),
            pltpu.VMEM((zs * rows_a, chunk), BF16),
            pltpu.VMEM((zs * rows_b, chunk), BF16),
            pltpu.VMEM((zs * rows_b, chunk), BF16),
            pltpu.VMEM((2 * spare, chunk), F32),
            pltpu.VMEM((2 * spare, chunk), BF16),
            pltpu.VMEM((2 * spare, chunk), BF16),
            pltpu.VMEM((1, 128), F32),
            pltpu.VMEM((zs, 1, 128), F32),
            pltpu.VMEM((1, 128), F32),
            pltpu.VMEM((xs - 1, 1, 128), F32),
            pltpu.VMEM((count, hidden), F32),
            dma((10,)),
            dma,
            dma((groups,)),
            dma,
            dma((groups,)),
            dma,
            dma((groups,)),
            dma,
            dma,
            dma,
            dma((groups,)),
            dma,
            dma,
            dma,
            dma((groups,)),
            dma,
            dma((zs // 4,)),
            dma,
            dma,
            dma((4,)),
        ],
        compiler_params=pltpu.CompilerParams(
            collective_id=0, has_side_effects=True, vmem_limit_bytes=VMEM_LIMIT
        ),
    )(
        decode_adapter_index.reshape(1, count),
        adapter_storage_index.reshape(1, -1),
        adapter_storage_index,
        block_adapter_index,
        block_live_count,
        decode_input_rows,
        learner_input_rows,
        learner_gradient,
        adapter_down_weight.reshape(held * rank, width),
        adapter_up_weight.reshape(held * rank, hidden),
    )
    def padded():
        return padded_exchange(
            decode_input_rows,
            decode_adapter_index,
            adapter_storage_index,
            adapter_down_weight.reshape(held * rank, width),
            adapter_up_weight.reshape(held * rank, hidden),
        )

    delta = lax.cond(flag[0] > 0, padded, lambda: delta)
    return delta, down.reshape(held, rank, width), up.reshape(held, rank, hidden)


def solution(mesh):
    in_specs = (
        P("dp", "tensor"),
        P("dp"),
        P(),
        P("dp", "tensor"),
        P("dp", "tensor"),
        P("dp"),
        P("dp"),
        P("dp", None, "tensor"),
        P("dp", None, "tensor"),
    )
    out_specs = (P("dp", "tensor"), P("dp", None, "tensor"), P("dp", None, "tensor"))
    return jax.shard_map(local, mesh=mesh, in_specs=in_specs, out_specs=out_specs, check_vma=False)
```
